256 devices in a mesh: dp: 4 (over y_lo, core), blk: 8 (over z), head: 8 (over y_hi, x).
Axes of the slice: x: 4, y: 4 (y_hi: 2, y_lo: 2; y = y_hi * 2 + y_lo), z: 8, core: 2. Of those that a mesh axis runs over, the one named last changes fastest.
Arguments:
- video: bfloat16 [16384, 3072], P(('dp', 'blk'), 'head'), parts along dimension 0, may hold values from -10 to 10
- text: bfloat16 [4096, 3072], P(('dp', 'blk'), 'head'), parts along dimension 0, may hold values from -6 to 6
- shift: float32 [3072], replicated, may hold values from -3 to 3
- scale: float32 [3072], replicated, may hold values from -3 to 3
- gate: float32 [3072], replicated, may hold values from 1 to 6
- w_qkv: bfloat16 [3072, 9216], P('blk', 'head'), may hold values from -1 to 1
- w_out: bfloat16 [3072, 3072], P('head', 'blk'), may hold values from -0.109375 to 0.109375
- q_gain: float32 [128], replicated, may hold values from 1 to 7
- k_gain: float32 [128], replicated, may hold values from 1 to 7
- clip_lengths: int32 [16], P('dp'), parts along dimension 0, may hold values from 1 to 2048, 4096 in all
- text_owner: int32 [16], P('dp'), parts along dimension 0, may hold values from 0 to 3, each once
Outputs:
- video_out: bfloat16 [16384, 3072], P(('dp', 'blk'), 'head'), parts along dimension 0
- text_out: bfloat16 [4096, 3072], P(('dp', 'blk'), 'head'), parts along dimension 0
The draws below stay inside these ranges and needn't reach their ends.
There are 4 independent parts, one for each index of `dp`. The reference program is written for one: setup_inputs(seed, part) draws one part's arguments, and reference() takes and returns one part's arrays. A program takes and returns all parts, laid end to end along the dimension named above; an argument that names none is the same for every part. Nothing has to cross between parts.
Inputs may be any that keep to these rules, and one draw needn't show every extreme that they name: `clip_lengths`: the clip lengths sum to 4096; the longest is exactly 2048. `text_owner`: each clip owns exactly one block of text rows.
All inputs are finite; a program needn't handle non-finite values.
Results may differ from the reference program's by a relative error of at most 0.018.
The reference program's roundings to bfloat16 on the way (of `modulated` and `attended`) count: a program that leaves them out, or rounds other values in their place, can miss the bound.
Values may be sent and summed in bfloat16 or wider, within the bound.
A program may use at most 128 MiB of HBM per device.

```python
import math
import jax
import jax.numpy as jnp
import numpy as np
from jax import lax

D = 3072
HEADS = 24
HD = 128
CLIPS = 4
TXT = 256
SV = 4096
TEXT = 1024


def draw_video(key, part):
    key = jax.random.fold_in(key, 11)
    noise = jnp.clip(jax.random.normal(jax.random.fold_in(key, 1), (SV, D), jnp.float32), -6.0, 6.0)
    return noise.astype(jnp.bfloat16)


def draw_w_qkv(key, part):
    key = jax.random.fold_in(key, 12)
    base = jax.random.normal(jax.random.fold_in(key, 1), (D, HEADS, 3, HD), jnp.float32)
    return jnp.clip(base * D ** (-0.5), -1.0, 1.0).reshape(D, 3 * HEADS * HD).astype(jnp.bfloat16)


def draw_q_gain(key, part):
    key = jax.random.fold_in(key, 13)
    spread = jax.random.uniform(key, (HD,), jnp.float32)
    return jnp.exp(spread * math.log(3.0))


def draw_k_gain(key, part):
    key = jax.random.fold_in(key, 14)
    spread = jax.random.uniform(key, (HD,), jnp.float32)
    return jnp.exp(spread * math.log(3.0))


def shard_levels(key, dims, split, least, top_value):
    factor_of, own = 1.0, jax.random.fold_in(key, 6)
    for axis_at, parts in split:
        heights = jnp.exp(jax.random.uniform(jax.random.fold_in(own, axis_at), (parts,), jnp.float32, least / len(split), top_value / len(split)))
        factor_of = factor_of * jnp.repeat(heights, dims[axis_at] // parts).reshape([-1 if axis == axis_at else 1 for axis in range(len(dims))])
    return factor_of


def split_up(number_of, total, reach, skew):
    weights = [(1 << 20) // math.isqrt(grade ** skew) + 1 for grade in range(2, number_of + 1)]
    rest, counts = total - reach - (number_of - 1), [1] * (number_of - 1)
    while rest > 0:
        free = [i for i in range(number_of - 1) if counts[i] < reach]
        whole, budget = sum([weights[i] for i in free]), rest
        for i in free:
            addition = min(reach - counts[i], max(1, budget * weights[i] // whole), rest)
            counts[i] = counts[i] + addition
            rest = rest - addition
    return np.array([reach] + counts)


def uneven_parts(stream_key, number_of, total, most, slope):
    if number_of == 2:
        one = jax.random.randint(stream_key, (), max(1, total - most), min(most, total - 1) + 1)
        return jnp.stack([one, total - one])
    sizes = jnp.asarray(split_up(number_of, total, most, slope), jnp.int32)
    twos = (number_of - 1) // 2
    source_of, sink = sizes[1:1 + 2 * twos:2], sizes[2:2 + 2 * twos:2]
    room = jnp.minimum(source_of - 1, most - sink)
    shifted = jax.random.randint(jax.random.fold_in(stream_key, 1), (twos,), 0, 1 << 20) % (room + 1)
    sizes = sizes.at[1:1 + 2 * twos:2].set(source_of - shifted).at[2:2 + 2 * twos:2].set(sink + shifted)
    return sizes[jax.random.permutation(jax.random.fold_in(stream_key, 2), number_of)]


def bell_draw(stream_key, extent, scale, bound, split=(), kind=jnp.bfloat16):
    loudness = shard_levels(stream_key, extent, split, -0.22, 0.18) if split else 1.0
    result = jax.random.normal(stream_key, extent, jnp.float32) * scale * loudness
    return jnp.minimum(jnp.maximum(result, -bound), bound).astype(kind)


def setup_inputs(seed: int = 0, part: int = 0) -> dict:
    splits = jax.random.split(jax.random.key(seed), 12)
    part_keys = jax.random.split(jax.random.fold_in(splits[11], part), 12)
    return {
        "video": draw_video(jax.random.fold_in(jax.random.fold_in(splits[11], part), 71), part),
        "text": bell_draw(part_keys[1], (TEXT, D), 1.0, 6.0, ((0, 8), (1, 8))),
        "shift": bell_draw(splits[2], (D,), 0.5, 3.0, (), jnp.float32),
        "scale": bell_draw(splits[3], (D,), 0.5, 3.0, (), jnp.float32),
        "gate": jnp.clip(jnp.exp(jax.random.uniform(splits[4], (D,), jnp.float32, math.log(1.0), math.log(6.0))), 1.0, 6.0),
        "w_qkv": draw_w_qkv(jax.random.fold_in(splits[11], 71), part),
        "w_out": bell_draw(splits[6], (HEADS * HD, D), (HEADS * HD) ** -0.5, 0.109375, ((0, 8), (1, 8))),
        "q_gain": draw_q_gain(jax.random.fold_in(splits[11], 71), part),
        "k_gain": draw_k_gain(jax.random.fold_in(splits[11], 71), part),
        "clip_lengths": uneven_parts(part_keys[9], CLIPS, SV, SV // 2, 1).astype(jnp.int32),
        "text_owner": jax.random.permutation(part_keys[10], CLIPS).astype(jnp.int32),
    }


def rotate(values, angles):
    half = values.shape[-1] // 2
    cosine = jnp.cos(angles)[:, None, :]
    sine = jnp.sin(angles)[:, None, :]
    first = values[..., :half]
    second = values[..., half:]
    return jnp.concatenate([first * cosine - second * sine, second * cosine + first * sine], axis=-1)

def rms_scale(values, gain):
    return values * lax.rsqrt(lax.optimization_barrier(jnp.mean(values * values, axis=-1, keepdims=True)) + 1e-06) * gain

def reference(video, text, shift, scale, gate, w_qkv, w_out, q_gain, k_gain, clip_lengths, text_owner):
    ends = jnp.cumsum(clip_lengths).astype(jnp.int32)
    starts = (ends - clip_lengths).astype(jnp.int32)
    video_index = jnp.arange(SV, dtype=jnp.int32)
    video_clip = lax.optimization_barrier(jnp.sum((video_index[:, None] >= ends[None, :]).astype(jnp.int32), axis=1)).astype(jnp.int32)
    video_place = (video_index - starts[video_clip]).astype(jnp.float32)
    text_clip = text_owner[jnp.arange(TEXT, dtype=jnp.int32) // TXT].astype(jnp.int32)
    clip_ids = jnp.concatenate([video_clip, text_clip])
    is_video = jnp.concatenate([jnp.ones((SV,), bool), jnp.zeros((TEXT,), bool)])
    places = jnp.concatenate([video_place, jnp.zeros((TEXT,), jnp.float32)])
    tokens = jnp.concatenate([video, text], axis=0).astype(jnp.float32)
    count = SV + TEXT
    mean = lax.optimization_barrier(jnp.mean(tokens, axis=1, keepdims=True))
    var = lax.optimization_barrier(jnp.mean((tokens - mean) ** 2, axis=1, keepdims=True))
    modulated = ((tokens - mean) * lax.rsqrt(var + 1e-06) * (1.0 + scale) + shift).astype(jnp.bfloat16)
    qkv = jnp.dot(modulated, w_qkv, preferred_element_type=jnp.float32).reshape(count, HEADS, 3, HD)
    freqs = 10000.0 ** (-2.0 * jnp.arange(HD // 2, dtype=jnp.float32) / HD)
    angles = places[:, None] * freqs[None, :]
    queries = rms_scale(qkv[:, :, 0], q_gain)
    keys = rms_scale(qkv[:, :, 1], k_gain)
    queries = jnp.where(is_video[:, None, None], rotate(queries, angles), queries).astype(jnp.bfloat16)
    keys = jnp.where(is_video[:, None, None], rotate(keys, angles), keys).astype(jnp.bfloat16)
    values = qkv[:, :, 2].astype(jnp.bfloat16)
    same_clip = clip_ids[:, None] == clip_ids[None, :]
    factor = 1.0 / HD ** 0.5

    def one_head(triple):
        head_q, head_k, head_v = triple
        scores = jnp.dot(head_q, head_k.T, preferred_element_type=jnp.float32) * factor
        scores = jnp.where(same_clip, scores, -1e+30)
        largest = lax.optimization_barrier(jnp.max(scores, axis=1, keepdims=True))
        weights = jnp.where(same_clip, jnp.exp(scores - largest), 0.0)
        total = lax.optimization_barrier(jnp.sum(weights, axis=1, keepdims=True))
        return jnp.dot(weights.astype(jnp.bfloat16), head_v, preferred_element_type=jnp.float32) / total
    per_head = lax.map(one_head, (queries.transpose(1, 0, 2), keys.transpose(1, 0, 2), values.transpose(1, 0, 2)))
    attended = per_head.transpose(1, 0, 2).reshape(count, HEADS * HD).astype(jnp.bfloat16)
    projected = jnp.dot(attended, w_out, preferred_element_type=jnp.float32)
    updated = (tokens + gate * projected).astype(jnp.bfloat16)
    return (updated[:SV], updated[SV:])
```

```python
import functools
import math

import jax
import jax.numpy as jnp
import numpy as np
from jax import lax
from jax.experimental import pallas as pl
from jax.experimental.pallas import tpu as pltpu
from jax.sharding import PartitionSpec as P

MESH = pl.DeviceIdType.MESH
BF = jnp.bfloat16
F32 = jnp.float32
ROWS = 640
VROWS = 512
WIDTH = 384
HD = 128
TILE = 128
TXT = 256


def remote(src, dst, send_sem, recv_sem, device):
    return pltpu.make_async_remote_copy(
        src_ref=src,
        dst_ref=dst,
        send_sem=send_sem,
        recv_sem=recv_sem,
        device_id=device,
        device_id_type=MESH,
    )


def greet(devices):
    barrier = pltpu.get_barrier_semaphore()
    for device in devices:
        pl.semaphore_signal(barrier, inc=1, device_id=device, device_id_type=MESH)
    pl.semaphore_wait(barrier, len(devices))


def project_kernel(
    video,
    text,
    w_qkv,
    w_out,
    shift,
    scale,
    q_gain,
    k_gain,
    freqs,
    lengths,
    q_out,
    kv_out,
    wo_out,
    tok,
    mod,
    wbuf,
    ring,
    wo,
    cos_t,
    sin_t,
    local_sem,
    tok_recv,
    tok_send,
    left_recv,
    right_recv,
    right_send,
    left_send,
    sib_recv,
    sib_send,
    swap_recv,
    swap_send,
    pair_recv,
    pair_send,
):
    dp, z, head = lax.axis_index("dp"), lax.axis_index("blk"), lax.axis_index("head")
    core = lax.rem(dp, 2)
    yh, x = head // 4, lax.rem(head, 4)
    sibling = (dp + 1 - 2 * core, z, head)
    up, down = (dp, lax.rem(z + 1, 8), head), (dp, lax.rem(z + 7, 8), head)
    xs = [lax.rem(x + d, 4) for d in range(4)]
    slot = [[yh * 4 + xs[d] for d in range(4)], [(1 - yh) * 4 + xs[d] for d in range(4)]]
    right, left, over = (dp, z, slot[0][1]), (dp, z, slot[0][3]), (dp, z, slot[1][0])
    greet([(dp, z, lax.rem(head + d, 8)) for d in range(1, 8)] + [up, down, sibling])

    sends = []

    def send(copy):
        copy.start()
        sends.append(copy)

    def cols_of(h):
        return pl.ds(pl.multiple_of(h * WIDTH, WIDTH), WIDTH)

    def tok_at(h, t, half=None):
        first, count = t * TILE, TILE
        if half is not None:
            first, count = first + half * (TILE // 2), TILE // 2
        return tok.at[pl.ds(first, count), cols_of(h)]

    def own_tile(t):
        return video.at[pl.ds(t * TILE, TILE)] if t < 4 else text.at[pl.ds(0, TILE)]

    def tok_sem(flip, dx, t, half):
        return tok_recv.at[flip, dx, t, half]

    send_count = [0]

    def tok_copy(src, h, t, half, flip, dx, device):
        index = send_count[0]
        send_count[0] += 1
        send(
            remote(
                src,
                tok_at(h, t, half),
                tok_send.at[index],
                tok_sem(flip, dx, t, half or 0),
                device,
            )
        )

    def tok_wait(flip, dx, t, half=None):
        ref = tok_at(slot[flip][dx], t, half)
        pltpu.make_async_copy(ref, ref, tok_sem(flip, dx, t, half or 0)).wait()

    def w_at(block, p, half=None):
        if p >= 6:
            first, count = (0, 64) if half is None else (half * 32, 32)
            return ring.at[block, p - 6, pl.ds(first, count)]
        first, count = (0, 192) if half is None else (half * 96, 96)
        rows = pl.ds(pl.multiple_of(block * WIDTH + core * 192 + first, 32), count)
        return wbuf.at[rows, w_cols(p)]

    def w_cols(p):
        return pl.ds(384 * p + 128, 256) if p < 3 else pl.ds(384 * (p - 3), 128)

    def own_piece(p):
        if p >= 6:
            return w_out.at[pl.ds(pl.multiple_of((p - 6) * 128 + core * 64, 64), 64)]
        return w_qkv.at[pl.ds(pl.multiple_of(core * 192, 192), 192), w_cols(p)]

    def ring_first(p):
        send(remote(own_piece(p), w_at(z, p), right_send.at[p, 0], left_recv.at[p, 0], up))
        send(remote(own_piece(p), w_at(z, p), left_send.at[p, 0], right_recv.at[p, 0], down))

    def swap(block, p):
        hh = p - 6
        target = wo.at[hh, head, core]

        @pl.when(block != head)
        def _():
            remote(
                ring.at[block, hh],
                target,
                swap_send.at[hh, block],
                swap_recv.at[hh, head],
                (dp, z, block),
            ).start()

        @pl.when(block == head)
        def _():
            pltpu.make_async_copy(ring.at[block, hh], target, swap_recv.at[hh, head]).start()

    def ring_step(p, s):
        lo, hi = lax.rem(z + 8 - s, 8), lax.rem(z + s, 8)
        half_a, half_b = (0, 1) if s == 4 else (None, None)
        ref = w_at(lo, p, half_a)
        pltpu.make_async_copy(ref, ref, left_recv.at[p, s - 1]).wait()
        if s < 4:
            src = w_at(lo, p, 0 if s == 3 else None)
            send(remote(src, src, right_send.at[p, s], left_recv.at[p, s], up))
        ref = w_at(hi, p, half_b)
        pltpu.make_async_copy(ref, ref, right_recv.at[p, s - 1]).wait()
        if s < 4:
            src = w_at(hi, p, 1 if s == 3 else None)
            send(remote(src, src, left_send.at[p, s], right_recv.at[p, s], down))
        if p < 6:
            for i, (block, half) in enumerate(((lo, half_a), (hi, half_b))):
                ref = w_at(block, p, half)
                k = 2 * (s - 1) + i
                send(remote(ref, ref, sib_send.at[p, k], sib_recv.at[p, k], sibling))
        elif s < 4:
            swap(lo, p)
            swap(hi, p)
        else:
            swap(lo, p)

    def sib_wait(p):
        for s in range(1, 5):
            for i in range(2):
                count = 96 if s == 4 else 192
                block = lax.rem(z + 8 - s, 8) if i == 0 else lax.rem(z + s, 8)
                first = i * 96 if s == 4 else 0
                rows = pl.ds(
                    pl.multiple_of(block * WIDTH + (1 - core) * 192 + first, 32), count
                )
                ref = wbuf.at[rows, w_cols(p)]
                pltpu.make_async_copy(ref, ref, sib_recv.at[p, 2 * (s - 1) + i]).wait()

    own = [
        pltpu.make_async_copy(video, tok.at[pl.ds(0, VROWS), cols_of(head)], local_sem.at[0]),
        pltpu.make_async_copy(
            text, tok.at[pl.ds(VROWS, ROWS - VROWS), cols_of(head)], local_sem.at[1]
        ),
        pltpu.make_async_copy(
            w_qkv, wbuf.at[pl.ds(pl.multiple_of(z * WIDTH, WIDTH), WIDTH)], local_sem.at[2]
        ),
    ] + [
        pltpu.make_async_copy(own_piece(p), w_at(z, p), local_sem.at[3 + p - 6]) for p in (6, 7, 8)
    ]
    for p in range(3):
        ring_first(p)
    for t in range(5):
        tok_copy(own_tile(t), head, t, None, 1, 0, over)
        tok_copy(own_tile(t), head, t, None, 0, 3, right)
        tok_copy(own_tile(t), head, t, None, 0, 1, left)
    for copy in own:
        copy.start()

    e0 = lengths[0]
    e1 = e0 + lengths[1]
    e2 = e1 + lengths[2]
    row = lax.broadcasted_iota(jnp.int32, (ROWS, HD), 0)
    place = z * VROWS + row
    start = jnp.where(place >= e0, e0, 0)
    start = jnp.where(place >= e1, e1, start)
    start = jnp.where(place >= e2, e2, start)
    place = jnp.where(row < VROWS, place - start, 0).astype(F32)
    angle = place * freqs[...]
    lane = lax.broadcasted_iota(jnp.int32, (ROWS, HD), 1)

    def wait_x1(t):
        for dx, half, device, far in ((3, 0, right, 2), (1, 1, left, 2)):
            tok_wait(0, dx, t)
            h = slot[0][dx]
            tok_copy(tok_at(h, t, half), h, t, half, 0, far, device)
            if t >= 3:
                tok_copy(tok_at(h, t), h, t, None, 1, dx, over)

    for t in range(3):
        tok_wait(1, 0, t)
        h = slot[1][0]
        tok_copy(tok_at(h, t), h, t, None, 1, 3, right)
        tok_copy(tok_at(h, t), h, t, None, 1, 1, left)
        ring_step(t, 1)
    cos_t[...] = jnp.cos(angle)
    sin_t[...] = jnp.where(lane < HD // 2, -jnp.sin(angle), jnp.sin(angle))
    for t in range(5):
        wait_x1(t)
        if t >= 2:
            ring_step(t - 2, 2)
    for t in range(3):
        for dx, half, device in ((3, 0, right), (1, 1, left)):
            tok_wait(1, dx, t)
            h = slot[1][dx]
            tok_copy(tok_at(h, t, half), h, t, half, 1, 2, device)
        ring_step(t, 3)
    for p in range(3, 9):
        ring_first(p)
    for t in (3, 4, 0, 1, 2):
        for half in range(2):
            tok_wait(0, 2, t, half)
        if t >= 3:
            h = slot[0][2]
            for half in range(2):
                tok_copy(tok_at(h, t, half), h, t, half, 1, 2, over)
        if t < 3:
            ring_step(t, 4)
    for p in range(3, 9):
        ring_step(p, 1)
    for t in range(3):
        for half in range(2):
            tok_wait(1, 2, t, half)
    for t in (3, 4):
        tok_wait(1, 0, t)
        tok_wait(1, 1, t)
        tok_wait(1, 3, t)
        for half in range(2):
            tok_wait(1, 2, t, half)
    for copy in own:
        copy.wait()
    for p in (6, 7, 8):
        swap(z, p)

    def normalise(first, count):
        @pl.loop(0, count)
        def _(i):
            rows = pl.ds(pl.multiple_of(first + i * 16, 16), 16)
            value = tok[rows, :].astype(F32)
            mean = jnp.sum(value, axis=1, keepdims=True) * (1.0 / 3072.0)
            value = value - mean
            var = jnp.sum(value * value, axis=1, keepdims=True) * (1.0 / 3072.0)
            value = value * lax.rsqrt(var + 1e-06) * (1.0 + scale[...]) + shift[...]
            mod[rows, :] = value.astype(BF)

    def rms_rope(value, gain):
        mean = jnp.sum(value * value, axis=1, keepdims=True) * (1.0 / HD)
        value = value * lax.rsqrt(mean + 1e-06) * gain
        return value * cos_t[...] + pltpu.roll(value, HD // 2, 1) * sin_t[...]

    normalise(0, 40)
    for p in range(3, 9):
        ring_step(p, 2)
    for p in range(3):
        sib_wait(p)

    @pl.loop(0, 3)
    def _(h):
        cols = pl.ds(pl.multiple_of(h * 384 + 128, 128), 256)
        kv = jnp.dot(mod[...], wbuf[:, cols], preferred_element_type=F32)
        kv_out[h, :, 0:HD] = rms_rope(kv[:, 0:HD], k_gain[...]).astype(BF)
        kv_out[h, :, HD : 2 * HD] = kv[:, HD : 2 * HD].astype(BF)

    for s in (3, 4):
        for p in range(3, 9):
            ring_step(p, s)
    for p in range(3, 6):
        sib_wait(p)

    for hh in range(3):
        for d in range(8):
            src = lax.rem(head + d, 8)
            ref = wo.at[hh, src, core]
            pltpu.make_async_copy(ref, ref, swap_recv.at[hh, src]).wait()
        ref = wo.at[hh, :, core]
        send(remote(ref, ref, pair_send.at[hh], pair_recv.at[hh], sibling))

    @pl.loop(0, 3)
    def _(h):
        cols = pl.ds(pl.multiple_of(h * 384, 128), 128)
        q = jnp.dot(mod[...], wbuf[:, cols], preferred_element_type=F32)
        q_out[h] = rms_rope(q, q_gain[...]).astype(BF)

    for hh in range(3):
        ref = wo.at[hh, :, 1 - core]
        pltpu.make_async_copy(ref, ref, pair_recv.at[hh]).wait()
    done = pltpu.make_async_copy(wo, wo_out, local_sem.at[6])
    done.start()
    for hh in range(3):
        for d in range(1, 8):
            block = lax.rem(head + d, 8)
            remote(
                ring.at[block, hh],
                wo.at[hh, head, core],
                swap_send.at[hh, block],
                swap_recv.at[hh, head],
                (dp, z, block),
            ).wait_send()
    for copy in sends:
        copy.wait_send()
    done.wait()


def attend_kernel(
    q,
    kv_in,
    wo,
    video,
    text,
    gate,
    lengths,
    owners,
    video_out,
    text_out,
    kvbuf,
    att,
    proj,
    best,
    total,
    acc,
    q_clip,
    local_sem,
    left_recv,
    right_recv,
    right_send,
    left_send,
    att_recv,
    att_send,
):
    dp, z, head = lax.axis_index("dp"), lax.axis_index("blk"), lax.axis_index("head")
    up, down = (dp, lax.rem(z + 1, 8), head), (dp, lax.rem(z + 7, 8), head)
    peers = [(dp, z, lax.rem(head + d, 8)) for d in range(1, 8)]
    greet(peers + [up, down])

    def own_sends(h):
        for i in range(2):
            remote(
                kv_in.at[h, i], kvbuf.at[h, z, i], right_send.at[h, i], left_recv.at[h, i], up
            ).start()
            remote(
                kv_in.at[h, 1 - i],
                kvbuf.at[h, z, 1 - i],
                left_send.at[h, i],
                right_recv.at[h, i],
                down,
            ).start()

    own_sends(0)
    own = pltpu.make_async_copy(kv_in, kvbuf.at[:, z], local_sem.at[0])
    own.start()

    e0 = lengths[0]
    e1 = e0 + lengths[1]
    e2 = e1 + lengths[2]

    def clips(place, is_video, owner):
        ids = (
            (place >= e0).astype(jnp.int32)
            + (place >= e1).astype(jnp.int32)
            + (place >= e2).astype(jnp.int32)
        )
        return jnp.where(is_video, ids, owner)

    row = lax.broadcasted_iota(jnp.int32, (ROWS, HD), 0)
    q_clip[...] = clips(z * VROWS + row, row < VROWS, owners[z // 2])
    proj[...] = jnp.zeros_like(proj)

    factor = math.log2(math.e) / math.sqrt(HD)

    def unit(h, b, first):
        keys = kvbuf[h, b, :, :, 0:HD].reshape(ROWS, HD)
        values = kvbuf[h, b, :, :, HD : 2 * HD].reshape(ROWS, HD)
        column = lax.broadcasted_iota(jnp.int32, (1, ROWS), 1)
        key_clip = clips(b * VROWS + column, column < VROWS, owners[b // 2])
        for t in range(5):
            rows = pl.ds(t * TILE, TILE)
            scores = lax.dot_general(
                q[h, rows, :], keys, (((1,), (1,)), ((), ())), preferred_element_type=F32
            )
            scores = jnp.where(q_clip[rows, 0:1] == key_clip, scores, -1e30)
            old = jnp.where(first, -1e30, best[rows, 0:1])
            newest = jnp.maximum(old, jnp.max(scores, axis=1, keepdims=True))
            weights = jnp.exp2((scores - newest) * factor)
            keep = jnp.exp2((old - newest) * factor)
            best[rows, :] = jnp.broadcast_to(newest, (TILE, HD))
            count = jnp.sum(weights, axis=1, keepdims=True)
            summed = jnp.dot(weights.astype(BF), values, preferred_element_type=F32)
            prior = jnp.where(first, 0.0, total[rows, 0:1])
            before = jnp.where(first, 0.0, acc[rows, :])
            total[rows, :] = jnp.broadcast_to(prior * keep + count, (TILE, HD))
            acc[rows, :] = before * keep + summed

    mine = pl.ds(pl.multiple_of(head * HD, HD), HD)

    def att_copy(h, d):
        part = att.at[h, :, mine]
        return remote(part, part, att_send.at[h, d], att_recv.at[h, 8 - d], peers[d - 1])

    def finish(h):
        att[h, :, mine] = (acc[...] / total[...]).astype(BF)
        for d in range(1, 8):
            att_copy(h, d).start()

    def out_project(h):
        for d in range(1, 8):
            src = lax.rem(head + d, 8)
            ref = att.at[h, :, pl.ds(pl.multiple_of(src * HD, HD), HD)]
            pltpu.make_async_copy(ref, ref, att_recv.at[h, d]).wait()
        proj[...] += jnp.dot(att[h], wo[h].reshape(8 * HD, WIDTH), preferred_element_type=F32)

    own.wait()

    def slot(t, carry):
        h, j = t // 7, lax.rem(t, 7)
        odd = lax.rem(j, 2)
        lo, hi = lax.rem(z + 7 - j // 2, 8), lax.rem(z + 1 + j // 2, 8)
        from_left, from_right = kvbuf.at[h, lo, odd], kvbuf.at[h, hi, 1 - odd]
        pltpu.make_async_copy(from_left, from_left, left_recv.at[h, j]).wait()

        @pl.when(j < 5)
        def _():
            remote(
                from_left, from_left, right_send.at[h, j + 2], left_recv.at[h, j + 2], up
            ).start()

        pltpu.make_async_copy(from_right, from_right, right_recv.at[h, j]).wait()

        @pl.when(j < 5)
        def _():
            remote(
                from_right, from_right, left_send.at[h, j + 2], right_recv.at[h, j + 2], down
            ).start()

        @pl.when((j == 4) & (h < 2))
        def _():
            own_sends(h + 1)

        @pl.when((j == 0) & (h > 0))
        def _():
            unit(h - 1, lax.rem(z + 4, 8), False)
            finish(h - 1)

        away = (j + 1) // 2
        unit(h, lax.rem(jnp.where(odd == 1, z + 8 - away, z + away), 8), j == 0)

        @pl.when((j == 5) & (h > 0))
        def _():
            out_project(h - 1)

        return carry

    lax.fori_loop(0, 21, slot, 0)
    unit(2, lax.rem(z + 4, 8), False)
    finish(2)
    out_project(2)
    scaled = gate[...] * proj[...]
    video_out[...] = (video[...].astype(F32) + scaled[0:VROWS]).astype(BF)
    text_out[...] = (text[...].astype(F32) + scaled[VROWS:ROWS]).astype(BF)

    def drain(t, carry):
        h, j = t // 7, lax.rem(t, 7)
        remote(
            kvbuf.at[h, z, 0], kvbuf.at[h, z, 0], right_send.at[h, j], left_recv.at[h, j], up
        ).wait_send()
        remote(
            kvbuf.at[h, z, 0], kvbuf.at[h, z, 0], left_send.at[h, j], right_recv.at[h, j], down
        ).wait_send()
        return carry

    lax.fori_loop(0, 21, drain, 0)
    for h in range(3):
        for d in range(1, 8):
            att_copy(h, d).wait_send()


def on_device(
    video, text, shift, scale, gate, w_qkv, w_out, q_gain, k_gain, clip_lengths, text_owner
):
    anywhere = pl.BlockSpec(memory_space=pl.ANY)
    vmem = pl.BlockSpec(memory_space=pltpu.VMEM)
    smem = pl.BlockSpec(memory_space=pltpu.SMEM)
    dma = pltpu.SemaphoreType.DMA
    exponents = np.arange(HD // 2, dtype=np.float64) * (-2.0 / HD)
    freqs = np.tile((10000.0**exponents).astype(np.float32), 2).reshape(1, HD)
    queries, key_values, wo = pl.pallas_call(
        project_kernel,
        name="project",
        out_shape=(
            jax.ShapeDtypeStruct((3, ROWS, HD), BF),
            jax.ShapeDtypeStruct((3, ROWS, 2 * HD), BF),
            jax.ShapeDtypeStruct((3, 8, 2, 64, WIDTH), BF),
        ),
        in_specs=[anywhere] * 4 + [vmem] * 5 + [smem],
        out_specs=(vmem, vmem, anywhere),
        scratch_shapes=[
            pltpu.VMEM((ROWS, 3072), BF),
            pltpu.VMEM((ROWS, 3072), BF),
            pltpu.VMEM((3072, 1152), BF),
            pltpu.VMEM((8, 3, 64, WIDTH), BF),
            pltpu.VMEM((3, 8, 2, 64, WIDTH), BF),
            pltpu.VMEM((ROWS, HD), F32),
            pltpu.VMEM((ROWS, HD), F32),
            dma((7,)),
            dma((2, 4, 5, 2)),
            dma((64,)),
            dma((9, 4)),
            dma((9, 4)),
            dma((9, 4)),
            dma((9, 4)),
            dma((6, 8)),
            dma((6, 8)),
            dma((3, 8)),
            dma((3, 8)),
            dma((3,)),
            dma((3,)),
        ],
        compiler_params=pltpu.CompilerParams(
            collective_id=1, has_side_effects=True, vmem_limit_bytes=52 * 2**20
        ),
    )(
        video,
        text,
        w_qkv,
        w_out,
        shift.reshape(1, -1),
        scale.reshape(1, -1),
        q_gain.reshape(1, HD),
        k_gain.reshape(1, HD),
        jnp.asarray(freqs),
        clip_lengths,
    )
    gate_here = lax.dynamic_slice_in_dim(gate, lax.axis_index("head") * WIDTH, WIDTH)
    return pl.pallas_call(
        attend_kernel,
        name="attend",
        out_shape=(
            jax.ShapeDtypeStruct((VROWS, WIDTH), BF),
            jax.ShapeDtypeStruct((ROWS - VROWS, WIDTH), BF),
        ),
        in_specs=[vmem, anywhere, vmem, vmem, vmem, vmem, smem, smem],
        out_specs=(vmem, vmem),
        scratch_shapes=[
            pltpu.VMEM((3, 8, 2, ROWS // 2, 2 * HD), BF),
            pltpu.VMEM((3, ROWS, 8 * HD), BF),
            pltpu.VMEM((ROWS, WIDTH), F32),
            pltpu.VMEM((ROWS, HD), F32),
            pltpu.VMEM((ROWS, HD), F32),
            pltpu.VMEM((ROWS, HD), F32),
            pltpu.VMEM((ROWS, HD), jnp.int32),
            dma((1,)),
            dma((3, 7)),
            dma((3, 7)),
            dma((3, 7)),
            dma((3, 7)),
            dma((3, 8)),
            dma((3, 8)),
        ],
        compiler_params=pltpu.CompilerParams(
            collective_id=2, has_side_effects=True, vmem_limit_bytes=52 * 2**20
        ),
    )(
        queries,
        key_values.reshape(3, 2, ROWS // 2, 2 * HD),
        wo,
        video,
        text,
        gate_here.reshape(1, WIDTH),
        clip_lengths,
        text_owner,
    )


def solution(mesh):
    return jax.shard_map(
        on_device,
        mesh=mesh,
        in_specs=(
            P(("dp", "blk"), "head"),
            P(("dp", "blk"), "head"),
            P(),
            P(),
            P(),
            P("blk", "head"),
            P("head", "blk"),
            P(),
            P(),
            P("dp"),
            P("dp"),
        ),
        out_specs=(P(("dp", "blk"), "head"), P(("dp", "blk"), "head")),
        check_vma=False,
    )
```

```python
import functools
import math

import jax
import jax.numpy as jnp
import numpy as np
from jax import lax
from jax.experimental import pallas as pl
from jax.experimental.pallas import tpu as pltpu
from jax.sharding import PartitionSpec as P

MESH = pl.DeviceIdType.MESH
BF = jnp.bfloat16
F32 = jnp.float32
ROWS = 640
VROWS = 512
WIDTH = 384
HD = 128
TILE = 128


def remote(src, dst, send_sem, recv_sem, device):
    return pltpu.make_async_remote_copy(
        src_ref=src,
        dst_ref=dst,
        send_sem=send_sem,
        recv_sem=recv_sem,
        device_id=device,
        device_id_type=MESH,
    )


def greet(devices):
    barrier = pltpu.get_barrier_semaphore()
    for device in devices:
        pl.semaphore_signal(barrier, inc=1, device_id=device, device_id_type=MESH)
    pl.semaphore_wait(barrier, len(devices))


PARTS = {"all": (0, 128, 0), "a": (0, 64, 0), "b": (64, 64, 1), "a0": (0, 32, 0), "a1": (32, 32, 2)}


def sublayer_kernel(
    video,
    text,
    w_qkv,
    w_out,
    shift_in,
    scale_in,
    gate_in,
    q_gain_in,
    k_gain_in,
    freqs_in,
    lengths,
    owners,
    video_out,
    text_out,
    tok,
    mod,
    wkv,
    wq,
    ring,
    wo,
    cos_t,
    sin_t,
    shift,
    scale,
    gate,
    q_gain,
    k_gain,
    freqs,
    q,
    kvbuf,
    att,
    proj,
    best,
    total,
    acc,
    q_clip,
    local_sem,
    tok_recv,
    tok_send,
    wl_recv,
    wr_recv,
    wr_send,
    wl_send,
    sib_recv,
    sib_send,
    ol_recv,
    or_recv,
    or_send,
    ol_send,
    swap_recv,
    swap_send,
    share_recv,
    share_send,
    left_recv,
    right_recv,
    right_send,
    left_send,
    att_recv,
    att_send,
    last_recv,
    last_send,
):
    dp, z, head = lax.axis_index("dp"), lax.axis_index("blk"), lax.axis_index("head")
    core = lax.rem(dp, 2)
    yh, x = head // 4, lax.rem(head, 4)
    sibling = (dp + 1 - 2 * core, z, head)
    mates = [sibling] + [
        (d, z, head) for d in (lax.rem(dp + 2, 4), lax.rem(dp + 2, 4) + 1 - 2 * core)
    ]
    up, down = (dp, lax.rem(z + 1, 8), head), (dp, lax.rem(z + 7, 8), head)
    xs = [lax.rem(x + d, 4) for d in range(4)]
    slot = [[yh * 4 + xs[d] for d in range(4)], [(1 - yh) * 4 + xs[d] for d in range(4)]]
    right, left, over = (dp, z, slot[0][1]), (dp, z, slot[0][3]), (dp, z, slot[1][0])
    peers = [(dp, z, lax.rem(head + d, 8)) for d in range(1, 8)]
    greet(peers + [up, down] + mates)

    sends = []

    def send(copy):
        copy.start()
        sends.append(copy)

    def landed(ref, sem):
        pltpu.make_async_copy(ref, ref, sem).wait()

    def cols_of(h):
        return pl.ds(pl.multiple_of(h * WIDTH, WIDTH), WIDTH)

    def tok_at(h, t, part):
        first, count, _ = PARTS[part]
        return tok.at[pl.ds(t * TILE + first, count), cols_of(h)]

    def own_tile(t):
        return video.at[pl.ds(t * TILE, TILE)] if t < 4 else text.at[pl.ds(0, TILE)]

    send_count = [0]

    def tok_copy(src, h, t, part, flip, dx, device):
        index = send_count[0]
        send_count[0] += 1
        arrival = tok_recv.at[flip, dx, t, PARTS[part][2]]
        send(remote(src, tok_at(h, t, part), tok_send.at[index], arrival, device))

    def tok_pass(h, t, part, flip, dx, device):
        tok_copy(tok_at(h, t, part), h, t, part, flip, dx, device)

    def tok_wait(flip, dx, t, part):
        landed(tok_at(slot[flip][dx], t, part), tok_recv.at[flip, dx, t, PARTS[part][2]])

    def stage0(t):
        tok_copy(own_tile(t), head, t, "all", 0, 3, right)
        tok_copy(own_tile(t), head, t, "all", 0, 1, left)
        tok_copy(own_tile(t), head, t, "all", 1, 0, over)

    def stage1(t):
        tok_wait(1, 0, t, "all")
        tok_pass(slot[1][0], t, "a", 1, 3, right)
        tok_pass(slot[1][0], t, "a", 1, 1, left)
        for dx, part, device in ((3, "a", right), (1, "b", left)):
            tok_wait(0, dx, t, "all")
            tok_pass(slot[0][dx], t, part, 0, 2, device)
            tok_pass(slot[0][dx], t, "b", 1, dx, over)

    def stage2(t):
        for dx, part, device in ((3, "a0", right), (1, "a1", left)):
            tok_wait(1, dx, t, "a")
            tok_pass(slot[1][dx], t, part, 1, 2, device)
        tok_wait(0, 2, t, "a")
        tok_wait(0, 2, t, "b")
        tok_pass(slot[0][2], t, "b", 1, 2, over)

    def stage3(t):
        for dx, part in ((2, "a0"), (2, "a1"), (1, "b"), (3, "b"), (2, "b")):
            tok_wait(1, dx, t, part)
        normalise(t)

    def normalise(t):
        @pl.loop(0, 8)
        def _(i):
            rows = pl.ds(pl.multiple_of(t * TILE + i * 16, 16), 16)
            value = tok[rows, :].astype(F32)
            mean = jnp.sum(value, axis=1, keepdims=True) * (1.0 / 3072.0)
            value = value - mean
            var = jnp.sum(value * value, axis=1, keepdims=True) * (1.0 / 3072.0)
            value = value * lax.rsqrt(var + 1e-06) * (1.0 + scale[...]) + shift[...]
            mod[rows, :] = value.astype(BF)

    def w_at(block, p, half=None, side=None):
        first, count = (0, 192) if half is None else (half * 96, 96)
        side = core if side is None else side
        rows = pl.ds(pl.multiple_of(block * WIDTH + side * 192 + first, 32), count)
        return wkv.at[rows, pl.ds(256 * p, 256)] if p < 3 else wq.at[rows, pl.ds(128 * p - 384, 128)]

    def w_cols(p):
        return pl.ds(384 * p + 128, 256) if p < 3 else pl.ds(384 * (p - 3), 128)

    def ring_first(p):
        src = w_qkv.at[pl.ds(pl.multiple_of(core * 192, 192), 192), w_cols(p)]
        send(remote(src, w_at(z, p), wr_send.at[p, 0], wl_recv.at[p, 0], up))
        send(remote(src, w_at(z, p), wl_send.at[p, 0], wr_recv.at[p, 0], down))

    def ring_step(p, s):
        lo, hi = lax.rem(z + 8 - s, 8), lax.rem(z + s, 8)
        half_a, half_b = (0, 1) if s == 4 else (None, None)
        landed(w_at(lo, p, half_a), wl_recv.at[p, s - 1])
        if s < 4:
            src = w_at(lo, p, 0 if s == 3 else None)
            send(remote(src, src, wr_send.at[p, s], wl_recv.at[p, s], up))
        landed(w_at(hi, p, half_b), wr_recv.at[p, s - 1])
        if s < 4:
            src = w_at(hi, p, 1 if s == 3 else None)
            send(remote(src, src, wl_send.at[p, s], wr_recv.at[p, s], down))
        for i, (block, half) in enumerate(((lo, half_a), (hi, half_b))):
            ref = w_at(block, p, half)
            k = 2 * (s - 1) + i
            send(remote(ref, ref, sib_send.at[p, k], sib_recv.at[p, k], sibling))

    def sib_wait(p):
        for s in range(1, 5):
            for i in range(2):
                block = lax.rem(z + 8 - s, 8) if i == 0 else lax.rem(z + s, 8)
                ref = w_at(block, p, i if s == 4 else None, 1 - core)
                landed(ref, sib_recv.at[p, 2 * (s - 1) + i])

    quarter = w_out.at[:, pl.ds(pl.multiple_of(dp * 32, 32), 32)]

    def out_first():
        send(remote(quarter, ring.at[z], or_send.at[0], ol_recv.at[0], up))
        send(remote(quarter, ring.at[z], ol_send.at[0], or_recv.at[0], down))

    def out_at(block, half):
        return ring.at[block] if half is None else ring.at[block, :, pl.ds(half * 16, 16)]

    def out_sends(s):
        lo, hi = lax.rem(z + 8 - s, 8), lax.rem(z + s, 8)
        a, b = out_at(lo, 0 if s == 3 else None), out_at(hi, 1 if s == 3 else None)
        return (
            remote(a, a, or_send.at[s], ol_recv.at[s], up),
            remote(b, b, ol_send.at[s], or_recv.at[s], down),
        )

    def out_step(s):
        lo, hi = lax.rem(z + 8 - s, 8), lax.rem(z + s, 8)
        landed(out_at(lo, 0 if s == 4 else None), ol_recv.at[s - 1])
        landed(out_at(hi, 1 if s == 4 else None), or_recv.at[s - 1])
        if s < 4:
            for copy in out_sends(s):
                send(copy)

    def swap_copy(d):
        block = lax.rem(head + d, 8)
        target = wo.at[:, head, dp]
        return remote(
            ring.at[block], target, swap_send.at[d], swap_recv.at[8 - d], (dp, z, block)
        )

    swap_own = pltpu.make_async_copy(ring.at[head], wo.at[:, head, dp], swap_recv.at[0])

    def swap():
        for d in range(1, 8):
            swap_copy(d).start()
        swap_own.start()

    def share_copy(i):
        part = wo.at[:, :, mates[1][0] if i == 2 else dp]
        return remote(part, part, share_send.at[i], share_recv.at[i], mates[i % 2])

    def share():
        for d in range(8):
            landed(wo.at[:, lax.rem(head + d, 8), dp], swap_recv.at[d])
        for i in range(2):
            share_copy(i).start()

    def share_on():
        landed(wo.at[:, :, mates[1][0]], share_recv.at[1])
        share_copy(2).start()

    def share_wait():
        landed(wo.at[:, :, mates[0][0]], share_recv.at[0])
        landed(wo.at[:, :, mates[2][0]], share_recv.at[2])

    own = [
        pltpu.make_async_copy(video, tok.at[pl.ds(0, VROWS), cols_of(head)], local_sem.at[0]),
        pltpu.make_async_copy(
            text, tok.at[pl.ds(VROWS, ROWS - VROWS), cols_of(head)], local_sem.at[1]
        ),
        pltpu.make_async_copy(quarter, ring.at[z], local_sem.at[2]),
    ]
    block_rows = pl.ds(pl.multiple_of(z * WIDTH, WIDTH), WIDTH)
    for p in range(6):
        target = wkv.at[:, pl.ds(256 * p, 256)] if p < 3 else wq.at[:, pl.ds(128 * p - 384, 128)]
        own.append(
            pltpu.make_async_copy(
                w_qkv.at[:, w_cols(p)], target.at[block_rows], local_sem.at[3 + p]
            )
        )
    small = [
        pltpu.make_async_copy(a, b, local_sem.at[9 + i])
        for i, (a, b) in enumerate(
            (
                (freqs_in, freqs),
                (shift_in, shift),
                (scale_in, scale),
                (q_gain_in, q_gain),
                (k_gain_in, k_gain),
                (gate_in.at[:, cols_of(head)], gate),
            )
        )
    ]
    for p in range(6):
        ring_first(p)
    out_first()
    for t in range(3):
        stage0(t)
    for copy in small + own:
        copy.start()
    for copy in small:
        copy.wait()

    e0 = lengths[0]
    e1 = e0 + lengths[1]
    e2 = e1 + lengths[2]

    def clips(place, is_video, owner):
        ids = (
            (place >= e0).astype(jnp.int32)
            + (place >= e1).astype(jnp.int32)
            + (place >= e2).astype(jnp.int32)
        )
        return jnp.where(is_video, ids, owner)

    def tables(t):
        rows = pl.ds(t * TILE, TILE)
        row = lax.broadcasted_iota(jnp.int32, (TILE, HD), 0) + t * TILE
        place = z * VROWS + row
        q_clip[rows, :] = clips(place, row < VROWS, owners[z // 2])
        start = jnp.where(place >= e0, e0, 0)
        start = jnp.where(place >= e1, e1, start)
        start = jnp.where(place >= e2, e2, start)
        place = jnp.where(row < VROWS, place - start, 0).astype(F32)
        angle = place * freqs[...]
        lane = lax.broadcasted_iota(jnp.int32, (TILE, HD), 1)
        sine = jnp.sin(angle)
        cos_t[rows, :] = jnp.cos(angle)
        sin_t[rows, :] = jnp.where(lane < HD // 2, -sine, sine)

    def rms_rope(value, gain):
        mean = jnp.sum(value * value, axis=1, keepdims=True) * (1.0 / HD)
        value = value * lax.rsqrt(mean + 1e-06) * gain
        return value * cos_t[...] + pltpu.roll(value, HD // 2, 1) * sin_t[...]

    def ring_steps(s, *pieces):
        for p in pieces:
            if p == 6:
                out_step(s)
            else:
                ring_step(p, s)

    tables(0)
    stage1(0)
    stage0(3)
    ring_steps(1, 0, 1)
    tables(1)
    stage1(1)
    stage2(0)
    stage0(4)
    ring_steps(1, 2, 3)
    tables(2)
    for copy in own:
        copy.wait()
    stage1(2)
    stage2(1)
    ring_steps(1, 4, 5, 6)
    stage3(0)
    tables(3)
    stage1(3)
    stage2(2)
    ring_steps(2, 0, 1, 2)
    stage3(1)
    tables(4)
    stage1(4)
    stage2(3)
    ring_steps(2, 3, 4, 5, 6)
    stage3(2)
    stage2(4)
    ring_steps(3, 0, 1, 2)
    stage3(3)
    ring_steps(3, 3, 4, 5, 6)
    stage3(4)
    ring_steps(4, 0, 1, 2)
    sib_wait(0)

    def own_sends(h):
        for i in range(2):
            a, b = kvbuf.at[h, z, i], kvbuf.at[h, z, 1 - i]
            remote(a, a, right_send.at[h, i], left_recv.at[h, i], up).start()
            remote(b, b, left_send.at[h, i], right_recv.at[h, i], down).start()

    def pass_on(h, j):
        odd = lax.rem(j, 2)
        lo, hi = lax.rem(z + 7 - j // 2, 8), lax.rem(z + 1 + j // 2, 8)
        from_left, from_right = kvbuf.at[h, lo, odd], kvbuf.at[h, hi, 1 - odd]
        landed(from_left, left_recv.at[h, j])

        @pl.when(j < 5)
        def _():
            remote(
                from_left, from_left, right_send.at[h, j + 2], left_recv.at[h, j + 2], up
            ).start()

        landed(from_right, right_recv.at[h, j])

        @pl.when(j < 5)
        def _():
            remote(
                from_right, from_right, left_send.at[h, j + 2], right_recv.at[h, j + 2], down
            ).start()

    for h in range(3):
        kv = jnp.dot(mod[...], wkv[:, 256 * h : 256 * h + 256], preferred_element_type=F32)
        keys = rms_rope(kv[:, 0:HD], k_gain[...]).astype(BF)
        values = kv[:, HD : 2 * HD].astype(BF)
        for i in range(2):
            rows = slice(i * (ROWS // 2), (i + 1) * (ROWS // 2))
            kvbuf[h, z, i, :, 0:HD] = keys[rows]
            kvbuf[h, z, i, :, HD : 2 * HD] = values[rows]
        if h == 0:
            own_sends(0)
            ring_steps(4, 3, 4, 5, 6)
            swap()
            sib_wait(1)
            sib_wait(2)
        else:
            pass_on(0, h - 1)
    for p in range(3, 6):
        sib_wait(p)
    queries = jnp.dot(mod[...], wq[...], preferred_element_type=F32)
    for h in range(3):
        q[h] = rms_rope(queries[:, h * HD : (h + 1) * HD], q_gain[...]).astype(BF)
    proj[...] = jnp.zeros_like(proj)

    factor = math.log2(math.e) / math.sqrt(HD)
    mine = pl.ds(pl.multiple_of(head * HD, HD), HD)

    def unit(h, b, first, each=None):
        keys = kvbuf[h, b, :, :, 0:HD].reshape(ROWS, HD)
        values = kvbuf[h, b, :, :, HD : 2 * HD].reshape(ROWS, HD)
        column = lax.broadcasted_iota(jnp.int32, (1, ROWS), 1)
        key_clip = clips(b * VROWS + column, column < VROWS, owners[b // 2])
        for t in range(5):
            rows = pl.ds(t * TILE, TILE)
            scores = lax.dot_general(
                q[h, rows, :], keys, (((1,), (1,)), ((), ())), preferred_element_type=F32
            )
            scores = jnp.where(q_clip[rows, 0:1] == key_clip, scores, -1e30)
            old = jnp.where(first, -1e30, best[rows, 0:1])
            newest = jnp.maximum(old, jnp.max(scores, axis=1, keepdims=True))
            weights = jnp.exp2((scores - newest) * factor)
            keep = jnp.exp2((old - newest) * factor)
            best[rows, :] = jnp.broadcast_to(newest, (TILE, HD))
            count = jnp.sum(weights, axis=1, keepdims=True)
            summed = jnp.dot(weights.astype(BF), values, preferred_element_type=F32)
            prior = jnp.where(first, 0.0, total[rows, 0:1])
            before = jnp.where(first, 0.0, acc[rows, :])
            total[rows, :] = jnp.broadcast_to(prior * keep + count, (TILE, HD))
            acc[rows, :] = before * keep + summed
            if each is not None:
                each(t)

    def att_copy(h, d):
        part = att.at[h, :, mine]
        return remote(part, part, att_send.at[h, d], att_recv.at[h, 8 - d], peers[d - 1])

    def finish(h):
        att[h, :, mine] = (acc[...] / total[...]).astype(BF)
        for d in range(1, 8):
            att_copy(h, d).start()

    def from_peer(d):
        return pl.ds(pl.multiple_of(lax.rem(head + d, 8) * HD, HD), HD)

    def out_project(h):
        for d in range(1, 8):
            landed(att.at[h, :, from_peer(d)], att_recv.at[h, d])
        proj[...] += jnp.dot(att[h], wo[h].reshape(8 * HD, WIDTH), preferred_element_type=F32)

    def last_copy(t, d):
        part = att.at[2, pl.ds(t * TILE, TILE), mine]
        return remote(part, part, last_send.at[t, d], last_recv.at[t, 8 - d], peers[d - 1])

    def finish_tile(t):
        rows = pl.ds(t * TILE, TILE)
        att[2, rows, mine] = (acc[rows, :] / total[rows, :]).astype(BF)
        for d in range(1, 8):
            last_copy(t, d).start()

    def step(t, carry):
        h, j = t // 7, lax.rem(t, 7)
        odd = lax.rem(j, 2)

        @pl.when(t >= 2)
        def _():
            pass_on(h, j)

        @pl.when((j == 1) & (h < 2))
        def _():
            own_sends(h + 1)

        @pl.when(t == 1)
        def _():
            share()

        @pl.when(t == 8)
        def _():
            share_on()

        @pl.when((j == 0) & (h > 0))
        def _():
            unit(h - 1, lax.rem(z + 4, 8), False)
            finish(h - 1)

        away = (j + 1) // 2
        unit(h, lax.rem(jnp.where(odd == 1, z + 8 - away, z + away), 8), j == 0)

        @pl.when(t == 17)
        def _():
            share_wait()
            out_project(0)

        @pl.when(t == 19)
        def _():
            out_project(1)

        return carry

    lax.fori_loop(0, 21, step, 0)
    unit(2, lax.rem(z + 4, 8), False, finish_tile)
    weights_out = wo[2].reshape(8 * HD, WIDTH)
    for t in range(5):
        rows = pl.ds(t * TILE, TILE)
        for d in range(1, 8):
            landed(att.at[2, rows, from_peer(d)], last_recv.at[t, d])
        summed = proj[rows, :] + jnp.dot(att[2, rows, :], weights_out, preferred_element_type=F32)
        residual = tok[rows, cols_of(head)].astype(F32)
        result = (residual + gate[...] * summed).astype(BF)
        if t < 4:
            video_out[rows, :] = result
        else:
            text_out[...] = result

    def drain(t, carry):
        h, j = t // 7, lax.rem(t, 7)
        part = kvbuf.at[h, z, 0]
        remote(part, part, right_send.at[h, j], left_recv.at[h, j], up).wait_send()
        remote(part, part, left_send.at[h, j], right_recv.at[h, j], down).wait_send()
        return carry

    lax.fori_loop(0, 21, drain, 0)
    for d in range(1, 8):
        swap_copy(d).wait_send()
        for h in range(2):
            att_copy(h, d).wait_send()
        for t in range(5):
            last_copy(t, d).wait_send()
    for i in range(3):
        share_copy(i).wait_send()
    for copy in sends:
        copy.wait_send()


def on_device(
    video, text, shift, scale, gate, w_qkv, w_out, q_gain, k_gain, clip_lengths, text_owner
):
    anywhere = pl.BlockSpec(memory_space=pl.ANY)
    vmem = pl.BlockSpec(memory_space=pltpu.VMEM)
    smem = pl.BlockSpec(memory_space=pltpu.SMEM)
    dma = pltpu.SemaphoreType.DMA
    exponents = np.arange(HD // 2, dtype=np.float64) * (-2.0 / HD)
    freqs = np.tile((10000.0**exponents).astype(np.float32), 2).reshape(1, HD)
    return pl.pallas_call(
        sublayer_kernel,
        name="sublayer",
        out_shape=(
            jax.ShapeDtypeStruct((VROWS, WIDTH), BF),
            jax.ShapeDtypeStruct((ROWS - VROWS, WIDTH), BF),
        ),
        in_specs=[anywhere] * 10 + [smem] * 2,
        out_specs=(vmem, vmem),
        scratch_shapes=[
            pltpu.VMEM((ROWS, 3072), BF),
            pltpu.VMEM((ROWS, 3072), BF),
            pltpu.VMEM((3072, 768), BF),
            pltpu.VMEM((3072, 384), BF),
            pltpu.VMEM((8, 3, 32, WIDTH), BF),
            pltpu.VMEM((3, 8, 4, 32, WIDTH), BF),
            pltpu.VMEM((ROWS, HD), F32),
            pltpu.VMEM((ROWS, HD), F32),
            pltpu.VMEM((1, 3072), F32),
            pltpu.VMEM((1, 3072), F32),
            pltpu.VMEM((1, WIDTH), F32),
            pltpu.VMEM((1, HD), F32),
            pltpu.VMEM((1, HD), F32),
            pltpu.VMEM((1, HD), F32),
            pltpu.VMEM((3, ROWS, HD), BF),
            pltpu.VMEM((3, 8, 2, ROWS // 2, 2 * HD), BF),
            pltpu.VMEM((3, ROWS, 8 * HD), BF),
            pltpu.VMEM((ROWS, WIDTH), F32),
            pltpu.VMEM((ROWS, HD), F32),
            pltpu.VMEM((ROWS, HD), F32),
            pltpu.VMEM((ROWS, HD), F32),
            pltpu.VMEM((ROWS, HD), jnp.int32),
            dma((15,)),
            dma((2, 4, 5, 3)),
            dma((64,)),
            dma((6, 4)),
            dma((6, 4)),
            dma((6, 4)),
            dma((6, 4)),
            dma((6, 8)),
            dma((6, 8)),
            dma((4,)),
            dma((4,)),
            dma((4,)),
            dma((4,)),
            dma((8,)),
            dma((8,)),
            dma((3,)),
            dma((3,)),
            dma((3, 7)),
            dma((3, 7)),
            dma((3, 7)),
            dma((3, 7)),
            dma((2, 8)),
            dma((2, 8)),
            dma((5, 8)),
            dma((5, 8)),
        ],
        compiler_params=pltpu.CompilerParams(
            collective_id=1, has_side_effects=True, vmem_limit_bytes=60 * 2**20
        ),
    )(
        video,
        text,
        w_qkv,
        w_out.reshape(3, 128, WIDTH),
        shift.reshape(1, -1),
        scale.reshape(1, -1),
        gate.reshape(1, -1),
        q_gain.reshape(1, HD),
        k_gain.reshape(1, HD),
        jnp.asarray(freqs),
        clip_lengths,
        text_owner,
    )


def solution(mesh):
    return jax.shard_map(
        on_device,
        mesh=mesh,
        in_specs=(
            P(("dp", "blk"), "head"),
            P(("dp", "blk"), "head"),
            P(),
            P(),
            P(),
            P("blk", "head"),
            P("head", "blk"),
            P(),
            P(),
            P("dp"),
            P("dp"),
        ),
        out_specs=(P(("dp", "blk"), "head"), P(("dp", "blk"), "head")),
        check_vma=False,
    )
```

```python
import functools
import math

import jax
import jax.numpy as jnp
import numpy as np
from jax import lax
from jax.experimental import pallas as pl
from jax.experimental.pallas import tpu as pltpu
from jax.sharding import PartitionSpec as P

MESH = pl.DeviceIdType.MESH
BF = jnp.bfloat16
F32 = jnp.float32
ROWS = 640
VROWS = 512
WIDTH = 384
HD = 128
TILE = 128


def remote(src, dst, send_sem, recv_sem, device):
    return pltpu.make_async_remote_copy(
        src_ref=src,
        dst_ref=dst,
        send_sem=send_sem,
        recv_sem=recv_sem,
        device_id=device,
        device_id_type=MESH,
    )


def greet(devices):
    barrier = pltpu.get_barrier_semaphore()
    for device in devices:
        pl.semaphore_signal(barrier, inc=1, device_id=device, device_id_type=MESH)
    pl.semaphore_wait(barrier, len(devices))


PARTS = {
    "all": (0, 128, 0),
    "f0": (0, 64, 0),
    "f1": (64, 64, 1),
    "a": (0, 96, 0),
    "b": (96, 32, 1),
    "a0": (0, 48, 0),
    "a1": (48, 48, 2),
}


def sublayer_kernel(
    video,
    text,
    w_qkv,
    w_out,
    shift_in,
    scale_in,
    gate_in,
    q_gain_in,
    k_gain_in,
    freqs_in,
    lengths,
    owners,
    video_out,
    text_out,
    tok,
    mod,
    wkv,
    wq,
    ring,
    wo,
    cos_t,
    sin_t,
    shift,
    scale,
    gate,
    q_gain,
    k_gain,
    freqs,
    q_block,
    q,
    kvbuf,
    att,
    proj,
    best,
    total,
    acc,
    q_clip,
    local_sem,
    tok_recv,
    tok_send,
    wl_recv,
    wr_recv,
    wr_send,
    wl_send,
    sib_recv,
    sib_send,
    q_recv,
    q_send,
    ol_recv,
    or_recv,
    or_send,
    ol_send,
    swap_recv,
    swap_send,
    share_recv,
    share_send,
    left_recv,
    right_recv,
    right_send,
    left_send,
    att_recv,
    att_send,
    last_recv,
    last_send,
):
    dp, z, head = lax.axis_index("dp"), lax.axis_index("blk"), lax.axis_index("head")
    core = lax.rem(dp, 2)
    yh, x = head // 4, lax.rem(head, 4)
    sibling = (dp + 1 - 2 * core, z, head)
    mates = [sibling] + [
        (d, z, head) for d in (lax.rem(dp + 2, 4), lax.rem(dp + 2, 4) + 1 - 2 * core)
    ]
    up, down = (dp, lax.rem(z + 1, 8), head), (dp, lax.rem(z + 7, 8), head)
    xs = [lax.rem(x + d, 4) for d in range(4)]
    slot = [[yh * 4 + xs[d] for d in range(4)], [(1 - yh) * 4 + xs[d] for d in range(4)]]
    right, left, over = (dp, z, slot[0][1]), (dp, z, slot[0][3]), (dp, z, slot[1][0])
    peers = [(dp, z, lax.rem(head + d, 8)) for d in range(1, 8)]
    greet(peers + [up, down] + mates)

    sends = []

    def send(copy):
        copy.start()
        sends.append(copy)

    def landed(ref, sem):
        pltpu.make_async_copy(ref, ref, sem).wait()

    def cols_of(h):
        return pl.ds(pl.multiple_of(h * WIDTH, WIDTH), WIDTH)

    def tok_at(h, t, part):
        first, count, _ = PARTS[part]
        return tok.at[pl.ds(t * TILE + first, count), cols_of(h)]

    def own_tile(t):
        return video.at[pl.ds(t * TILE, TILE)] if t < 4 else text.at[pl.ds(0, TILE)]

    send_count = [0]

    def tok_copy(src, h, t, part, flip, dx, device):
        index = send_count[0]
        send_count[0] += 1
        arrival = tok_recv.at[flip, dx, t, PARTS[part][2]]
        send(remote(src, tok_at(h, t, part), tok_send.at[index], arrival, device))

    def tok_pass(h, t, part, flip, dx, device):
        tok_copy(tok_at(h, t, part), h, t, part, flip, dx, device)

    def tok_wait(flip, dx, t, part):
        landed(tok_at(slot[flip][dx], t, part), tok_recv.at[flip, dx, t, PARTS[part][2]])

    def stage0(t):
        tok_copy(own_tile(t), head, t, "all", 0, 3, right)
        tok_copy(own_tile(t), head, t, "all", 0, 1, left)
        tok_copy(own_tile(t), head, t, "all", 1, 0, over)

    def stage1(t):
        tok_wait(1, 0, t, "all")
        tok_pass(slot[1][0], t, "a", 1, 3, right)
        tok_pass(slot[1][0], t, "a", 1, 1, left)
        for dx, part, device in ((3, "f0", right), (1, "f1", left)):
            tok_wait(0, dx, t, "all")
            tok_pass(slot[0][dx], t, part, 0, 2, device)
            tok_pass(slot[0][dx], t, "b", 1, dx, over)

    def stage2(t):
        for dx, part, device in ((3, "a0", right), (1, "a1", left)):
            tok_wait(1, dx, t, "a")
            tok_pass(slot[1][dx], t, part, 1, 2, device)
        tok_wait(0, 2, t, "f0")
        tok_wait(0, 2, t, "f1")
        tok_pass(slot[0][2], t, "b", 1, 2, over)

    def stage3(t):
        for dx, part in ((2, "a0"), (2, "a1"), (1, "b"), (3, "b"), (2, "b")):
            tok_wait(1, dx, t, part)
        normalise(t)

    def normalise(t):
        @pl.loop(0, 8)
        def _(i):
            rows = pl.ds(pl.multiple_of(t * TILE + i * 16, 16), 16)
            value = tok[rows, :].astype(F32)
            mean = jnp.sum(value, axis=1, keepdims=True) * (1.0 / 3072.0)
            value = value - mean
            var = jnp.sum(value * value, axis=1, keepdims=True) * (1.0 / 3072.0)
            value = value * lax.rsqrt(var + 1e-06) * (1.0 + scale[...]) + shift[...]
            mod[rows, :] = value.astype(BF)

    def w_at(block, p, half=None, side=None):
        first, count = (0, 192) if half is None else (half * 96, 96)
        side = core if side is None else side
        rows = pl.ds(pl.multiple_of(block * WIDTH + side * 192 + first, 32), count)
        return wkv.at[rows, pl.ds(256 * p, 256)]

    def w_cols(p):
        return pl.ds(384 * p + 128, 256) if p < 3 else pl.ds(384 * (p - 3), 128)

    def ring_first(p):
        src = w_qkv.at[pl.ds(pl.multiple_of(core * 192, 192), 192), w_cols(p)]
        send(remote(src, w_at(z, p), wr_send.at[p, 0], wl_recv.at[p, 0], up))
        send(remote(src, w_at(z, p), wl_send.at[p, 0], wr_recv.at[p, 0], down))

    def ring_step(p, s):
        lo, hi = lax.rem(z + 8 - s, 8), lax.rem(z + s, 8)
        half_a, half_b = (0, 1) if s == 4 else (None, None)
        landed(w_at(lo, p, half_a), wl_recv.at[p, s - 1])
        if s < 4:
            src = w_at(lo, p, 0 if s == 3 else None)
            send(remote(src, src, wr_send.at[p, s], wl_recv.at[p, s], up))
        landed(w_at(hi, p, half_b), wr_recv.at[p, s - 1])
        if s < 4:
            src = w_at(hi, p, 1 if s == 3 else None)
            send(remote(src, src, wl_send.at[p, s], wr_recv.at[p, s], down))
        for i, (block, half) in enumerate(((lo, half_a), (hi, half_b))):
            ref = w_at(block, p, half)
            k = 2 * (s - 1) + i
            send(remote(ref, ref, sib_send.at[p, k], sib_recv.at[p, k], sibling))

    def sib_wait(p):
        for s in range(1, 5):
            for i in range(2):
                block = lax.rem(z + 8 - s, 8) if i == 0 else lax.rem(z + s, 8)
                ref = w_at(block, p, i if s == 4 else None, 1 - core)
                landed(ref, sib_recv.at[p, 2 * (s - 1) + i])

    def q_at(block, half, quarter):
        part = wq.at[block, quarter]
        return part if half is None else part.at[pl.ds(half * 48, 48)]

    def q_pair(s, quarter, split):
        lo, hi = lax.rem(z + 8 - s, 8), lax.rem(z + s, 8)
        return q_at(lo, 0 if split else None, quarter), q_at(hi, 1 if split else None, quarter)

    def q_sends(s):
        a, b = q_pair(s, dp, s == 3)
        send(remote(a, a, wr_send.at[3, s], wl_recv.at[3, s], up))
        send(remote(b, b, wl_send.at[3, s], wr_recv.at[3, s], down))

    def q_step(s):
        a, b = q_pair(s, dp, s == 4)
        landed(a, wl_recv.at[3, s - 1])
        landed(b, wr_recv.at[3, s - 1])
        if s < 4:
            q_sends(s)
        for i in range(2):
            for k, ref in enumerate((a, b)):
                n = 2 * (s - 1) + k
                send(remote(ref, ref, q_send.at[i, n], q_recv.at[i, n], mates[i]))

    def q_on():
        for s in range(1, 5):
            for k, ref in enumerate(q_pair(s, mates[1][0], s == 4)):
                landed(ref, q_recv.at[1, 2 * (s - 1) + k])
        part = wq.at[:, mates[1][0]]
        send(remote(part, part, q_send.at[2, 0], q_recv.at[2, 0], sibling))

    def q_wait():
        for s in range(1, 5):
            for k, ref in enumerate(q_pair(s, sibling[0], s == 4)):
                landed(ref, q_recv.at[0, 2 * (s - 1) + k])
        landed(wq.at[:, mates[2][0]], q_recv.at[2, 0])

    quarter = w_out.at[:, pl.ds(pl.multiple_of(dp * 32, 32), 32)]

    def out_first():
        send(remote(quarter, ring.at[z], or_send.at[0], ol_recv.at[0], up))
        send(remote(quarter, ring.at[z], ol_send.at[0], or_recv.at[0], down))

    def out_at(block, half):
        return ring.at[block] if half is None else ring.at[block, :, pl.ds(half * 16, 16)]

    def out_sends(s):
        lo, hi = lax.rem(z + 8 - s, 8), lax.rem(z + s, 8)
        a, b = out_at(lo, 0 if s == 3 else None), out_at(hi, 1 if s == 3 else None)
        return (
            remote(a, a, or_send.at[s], ol_recv.at[s], up),
            remote(b, b, ol_send.at[s], or_recv.at[s], down),
        )

    def out_step(s):
        lo, hi = lax.rem(z + 8 - s, 8), lax.rem(z + s, 8)
        landed(out_at(lo, 0 if s == 4 else None), ol_recv.at[s - 1])
        landed(out_at(hi, 1 if s == 4 else None), or_recv.at[s - 1])
        if s < 4:
            for copy in out_sends(s):
                send(copy)

    def swap_copy(d):
        block = lax.rem(head + d, 8)
        target = wo.at[:, head, dp]
        return remote(
            ring.at[block], target, swap_send.at[d], swap_recv.at[8 - d], (dp, z, block)
        )

    swap_own = pltpu.make_async_copy(ring.at[head], wo.at[:, head, dp], swap_recv.at[0])

    def swap():
        for d in range(1, 8):
            swap_copy(d).start()
        swap_own.start()

    def share_copy(i):
        part = wo.at[:, :, mates[1][0] if i == 2 else dp]
        return remote(part, part, share_send.at[i], share_recv.at[i], mates[i % 2])

    def share():
        for d in range(8):
            landed(wo.at[:, lax.rem(head + d, 8), dp], swap_recv.at[d])
        for i in range(2):
            share_copy(i).start()

    def share_on():
        landed(wo.at[:, :, mates[1][0]], share_recv.at[1])
        share_copy(2).start()

    def share_wait():
        landed(wo.at[:, :, mates[0][0]], share_recv.at[0])
        landed(wo.at[:, :, mates[2][0]], share_recv.at[2])

    own = [
        pltpu.make_async_copy(video, tok.at[pl.ds(0, VROWS), cols_of(head)], local_sem.at[0]),
        pltpu.make_async_copy(
            text, tok.at[pl.ds(VROWS, ROWS - VROWS), cols_of(head)], local_sem.at[1]
        ),
        pltpu.make_async_copy(quarter, ring.at[z], local_sem.at[2]),
    ]
    block_rows = pl.ds(pl.multiple_of(z * WIDTH, WIDTH), WIDTH)
    own_queries, own_quarters = [], []
    for p in range(3):
        own.append(
            pltpu.make_async_copy(
                w_qkv.at[:, w_cols(p)],
                wkv.at[block_rows, pl.ds(256 * p, 256)],
                local_sem.at[3 + p],
            )
        )
        own_queries.append(
            pltpu.make_async_copy(
                w_qkv.at[:, w_cols(3 + p)],
                q_block.at[:, pl.ds(128 * p, 128)],
                local_sem.at[6 + p],
            )
        )
    for i, quarter_of in enumerate((dp, mates[0][0], mates[1][0])):
        rows = pl.ds(pl.multiple_of(quarter_of * 96, 96), 96)
        own_quarters.append(
            pltpu.make_async_copy(q_block.at[rows], wq.at[z, quarter_of], local_sem.at[15 + i])
        )
    small = [
        pltpu.make_async_copy(a, b, local_sem.at[9 + i])
        for i, (a, b) in enumerate(
            (
                (freqs_in, freqs),
                (shift_in, shift),
                (scale_in, scale),
                (q_gain_in, q_gain),
                (k_gain_in, k_gain),
                (gate_in.at[:, cols_of(head)], gate),
            )
        )
    ]
    for copy in own_queries:
        copy.start()
    for p in range(3):
        ring_first(p)
    for t in range(5):
        stage0(t)
    for copy in small + own:
        copy.start()
    for copy in small:
        copy.wait()

    def query_first():
        src = q_block.at[pl.ds(pl.multiple_of(dp * 96, 96), 96)]
        send(remote(src, wq.at[z, dp], wr_send.at[3, 0], wl_recv.at[3, 0], up))
        send(remote(src, wq.at[z, dp], wl_send.at[3, 0], wr_recv.at[3, 0], down))

    e0 = lengths[0]
    e1 = e0 + lengths[1]
    e2 = e1 + lengths[2]

    def clips(place, is_video, owner):
        ids = (
            (place >= e0).astype(jnp.int32)
            + (place >= e1).astype(jnp.int32)
            + (place >= e2).astype(jnp.int32)
        )
        return jnp.where(is_video, ids, owner)

    def tables(t):
        rows = pl.ds(t * TILE, TILE)
        row = lax.broadcasted_iota(jnp.int32, (TILE, HD), 0) + t * TILE
        place = z * VROWS + row
        q_clip[rows, :] = clips(place, row < VROWS, owners[z // 2])
        start = jnp.where(place >= e0, e0, 0)
        start = jnp.where(place >= e1, e1, start)
        start = jnp.where(place >= e2, e2, start)
        place = jnp.where(row < VROWS, place - start, 0).astype(F32)
        angle = place * freqs[...]
        lane = lax.broadcasted_iota(jnp.int32, (TILE, HD), 1)
        sine = jnp.sin(angle)
        cos_t[rows, :] = jnp.cos(angle)
        sin_t[rows, :] = jnp.where(lane < HD // 2, -sine, sine)

    def rms_rope(value, gain):
        mean = jnp.sum(value * value, axis=1, keepdims=True) * (1.0 / HD)
        value = value * lax.rsqrt(mean + 1e-06) * gain
        return value * cos_t[...] + pltpu.roll(value, HD // 2, 1) * sin_t[...]

    def ring_steps(s, *pieces):
        for p in pieces:
            if p == 4:
                out_step(s)
            elif p == 3:
                q_step(s)
            else:
                ring_step(p, s)

    for t in range(5):
        tables(t)
        stage1(t)
        if t < 3:
            ring_steps(1, t)
    for copy in own_queries:
        copy.wait()
    for copy in own_quarters:
        copy.start()
    query_first()
    out_first()
    for t in range(5):
        stage2(t)
        if t < 3:
            ring_steps(2, t)
    for copy in own + own_quarters:
        copy.wait()
    ring_steps(1, 3, 4)
    stage3(0)
    ring_steps(3, 0, 1, 2)
    stage3(1)
    ring_steps(2, 3, 4)
    stage3(2)
    ring_steps(4, 0, 1, 2)
    ring_steps(3, 3, 4)
    stage3(3)
    stage3(4)
    sib_wait(0)

    def own_sends(h):
        for i in range(2):
            a, b = kvbuf.at[h, z, i], kvbuf.at[h, z, 1 - i]
            remote(a, a, right_send.at[h, i], left_recv.at[h, i], up).start()
            remote(b, b, left_send.at[h, i], right_recv.at[h, i], down).start()

    def pass_on(h, j):
        odd = lax.rem(j, 2)
        lo, hi = lax.rem(z + 7 - j // 2, 8), lax.rem(z + 1 + j // 2, 8)
        from_left, from_right = kvbuf.at[h, lo, odd], kvbuf.at[h, hi, 1 - odd]
        landed(from_left, left_recv.at[h, j])

        @pl.when(j < 5)
        def _():
            remote(
                from_left, from_left, right_send.at[h, j + 2], left_recv.at[h, j + 2], up
            ).start()

        landed(from_right, right_recv.at[h, j])

        @pl.when(j < 5)
        def _():
            remote(
                from_right, from_right, left_send.at[h, j + 2], right_recv.at[h, j + 2], down
            ).start()

    for h in range(3):
        kv = jnp.dot(mod[...], wkv[:, 256 * h : 256 * h + 256], preferred_element_type=F32)
        keys = rms_rope(kv[:, 0:HD], k_gain[...]).astype(BF)
        values = kv[:, HD : 2 * HD].astype(BF)
        for i in range(2):
            rows = slice(i * (ROWS // 2), (i + 1) * (ROWS // 2))
            kvbuf[h, z, i, :, 0:HD] = keys[rows]
            kvbuf[h, z, i, :, HD : 2 * HD] = values[rows]
        if h == 0:
            own_sends(0)
            ring_steps(4, 3, 4)
            q_on()
            swap()
            sib_wait(1)
            sib_wait(2)
        elif h == 1:
            own_sends(1)
            pass_on(0, 0)
    q_wait()
    pass_on(0, 1)
    queries = jnp.dot(mod[...], wq[...].reshape(3072, WIDTH), preferred_element_type=F32)
    for h in range(3):
        q[h] = rms_rope(queries[:, h * HD : (h + 1) * HD], q_gain[...]).astype(BF)
    proj[...] = jnp.zeros_like(proj)

    factor = math.log2(math.e) / math.sqrt(HD)
    mine = pl.ds(pl.multiple_of(head * HD, HD), HD)

    def unit(h, b, first, each=None):
        keys = kvbuf[h, b, :, :, 0:HD].reshape(ROWS, HD)
        values = kvbuf[h, b, :, :, HD : 2 * HD].reshape(ROWS, HD)
        column = lax.broadcasted_iota(jnp.int32, (1, ROWS), 1)
        key_clip = clips(b * VROWS + column, column < VROWS, owners[b // 2])
        tiles = [pl.ds(t * TILE, TILE) for t in range(5)]
        scored = [
            lax.dot_general(
                q[h, rows, :], keys, (((1,), (1,)), ((), ())), preferred_element_type=F32
            )
            for rows in tiles
        ]
        weighed = []
        for rows, scores in zip(tiles, scored):
            scores = jnp.where(q_clip[rows, 0:1] == key_clip, scores, -1e30)
            old = jnp.where(first, -1e30, best[rows, 0:1])
            newest = jnp.maximum(old, jnp.max(scores, axis=1, keepdims=True))
            weights = jnp.exp2((scores - newest) * factor)
            best[rows, :] = jnp.broadcast_to(newest, (TILE, HD))
            weighed.append((weights, jnp.exp2((old - newest) * factor)))
        for t, (rows, (weights, keep)) in enumerate(zip(tiles, weighed)):
            count = jnp.sum(weights, axis=1, keepdims=True)
            summed = jnp.dot(weights.astype(BF), values, preferred_element_type=F32)
            prior = jnp.where(first, 0.0, total[rows, 0:1])
            before = jnp.where(first, 0.0, acc[rows, :])
            total[rows, :] = jnp.broadcast_to(prior * keep + count, (TILE, HD))
            acc[rows, :] = before * keep + summed
            if each is not None:
                each(t)

    def att_copy(h, d):
        part = att.at[h, :, mine]
        return remote(part, part, att_send.at[h, d], att_recv.at[h, 8 - d], peers[d - 1])

    def finish(h):
        att[h, :, mine] = (acc[...] / total[...]).astype(BF)
        for d in range(1, 8):
            att_copy(h, d).start()

    def from_peer(d):
        return pl.ds(pl.multiple_of(lax.rem(head + d, 8) * HD, HD), HD)

    def out_project(h):
        for d in range(1, 8):
            landed(att.at[h, :, from_peer(d)], att_recv.at[h, d])
        proj[...] += jnp.dot(att[h], wo[h].reshape(8 * HD, WIDTH), preferred_element_type=F32)

    def last_copy(t, d):
        part = att.at[2, pl.ds(t * TILE, TILE), mine]
        return remote(part, part, last_send.at[t, d], last_recv.at[t, 8 - d], peers[d - 1])

    def finish_tile(t):
        rows = pl.ds(t * TILE, TILE)
        att[2, rows, mine] = (acc[rows, :] / total[rows, :]).astype(BF)
        for d in range(1, 8):
            last_copy(t, d).start()

    def step(t, carry):
        h, j = t // 7, lax.rem(t, 7)
        odd = lax.rem(j, 2)

        @pl.when(t >= 2)
        def _():
            pass_on(h, j)

        @pl.when(t == 4)
        def _():
            own_sends(2)

        @pl.when(t == 1)
        def _():
            share()

        @pl.when(t == 8)
        def _():
            share_on()

        away = jnp.where(j == 6, 4, (j + 1) // 2)
        unit(h, lax.rem(jnp.where(odd == 1, z + 8 - away, z + away), 8), j == 0)

        @pl.when(j == 5)
        def _():
            unit(h, lax.rem(z + 3, 8), False)

        @pl.when(j == 6)
        def _():
            finish(h)

        @pl.when(t == 17)
        def _():
            share_wait()
            out_project(0)

        @pl.when(t == 19)
        def _():
            out_project(1)

        return carry

    lax.fori_loop(0, 20, step, 0)
    pass_on(2, 6)
    unit(2, lax.rem(z + 4, 8), False, finish_tile)
    weights_out = wo[2].reshape(8 * HD, WIDTH)
    for t in range(5):
        rows = pl.ds(t * TILE, TILE)
        for d in range(1, 8):
            landed(att.at[2, rows, from_peer(d)], last_recv.at[t, d])
        summed = proj[rows, :] + jnp.dot(att[2, rows, :], weights_out, preferred_element_type=F32)
        residual = tok[rows, cols_of(head)].astype(F32)
        result = (residual + gate[...] * summed).astype(BF)
        if t < 4:
            video_out[rows, :] = result
        else:
            text_out[...] = result

    def drain(t, carry):
        h, j = t // 7, lax.rem(t, 7)
        part = kvbuf.at[h, z, 0]
        remote(part, part, right_send.at[h, j], left_recv.at[h, j], up).wait_send()
        remote(part, part, left_send.at[h, j], right_recv.at[h, j], down).wait_send()
        return carry

    lax.fori_loop(0, 21, drain, 0)
    for d in range(1, 8):
        swap_copy(d).wait_send()
        for h in range(2):
            att_copy(h, d).wait_send()
        for t in range(5):
            last_copy(t, d).wait_send()
    for i in range(3):
        share_copy(i).wait_send()
    for copy in sends:
        copy.wait_send()


def on_device(
    video, text, shift, scale, gate, w_qkv, w_out, q_gain, k_gain, clip_lengths, text_owner
):
    anywhere = pl.BlockSpec(memory_space=pl.ANY)
    vmem = pl.BlockSpec(memory_space=pltpu.VMEM)
    smem = pl.BlockSpec(memory_space=pltpu.SMEM)
    dma = pltpu.SemaphoreType.DMA
    exponents = np.arange(HD // 2, dtype=np.float64) * (-2.0 / HD)
    freqs = np.tile((10000.0**exponents).astype(np.float32), 2).reshape(1, HD)
    return pl.pallas_call(
        sublayer_kernel,
        name="sublayer",
        out_shape=(
            jax.ShapeDtypeStruct((VROWS, WIDTH), BF),
            jax.ShapeDtypeStruct((ROWS - VROWS, WIDTH), BF),
        ),
        in_specs=[anywhere] * 10 + [smem] * 2,
        out_specs=(vmem, vmem),
        scratch_shapes=[
            pltpu.VMEM((ROWS, 3072), BF),
            pltpu.VMEM((ROWS, 3072), BF),
            pltpu.VMEM((3072, 768), BF),
            pltpu.VMEM((8, 4, 96, WIDTH), BF),
            pltpu.VMEM((8, 3, 32, WIDTH), BF),
            pltpu.VMEM((3, 8, 4, 32, WIDTH), BF),
            pltpu.VMEM((ROWS, HD), F32),
            pltpu.VMEM((ROWS, HD), F32),
            pltpu.VMEM((1, 3072), F32),
            pltpu.VMEM((1, 3072), F32),
            pltpu.VMEM((1, WIDTH), F32),
            pltpu.VMEM((1, HD), F32),
            pltpu.VMEM((1, HD), F32),
            pltpu.VMEM((1, HD), F32),
            pltpu.VMEM((WIDTH, WIDTH), BF),
            pltpu.VMEM((3, ROWS, HD), BF),
            pltpu.VMEM((3, 8, 2, ROWS // 2, 2 * HD), BF),
            pltpu.VMEM((3, ROWS, 8 * HD), BF),
            pltpu.VMEM((ROWS, WIDTH), F32),
            pltpu.VMEM((ROWS, HD), F32),
            pltpu.VMEM((ROWS, HD), F32),
            pltpu.VMEM((ROWS, HD), F32),
            pltpu.VMEM((ROWS, HD), jnp.int32),
            dma((18,)),
            dma((2, 4, 5, 3)),
            dma((64,)),
            dma((4, 4)),
            dma((4, 4)),
            dma((4, 4)),
            dma((4, 4)),
            dma((3, 8)),
            dma((3, 8)),
            dma((3, 8)),
            dma((3, 8)),
            dma((4,)),
            dma((4,)),
            dma((4,)),
            dma((4,)),
            dma((8,)),
            dma((8,)),
            dma((3,)),
            dma((3,)),
            dma((3, 7)),
            dma((3, 7)),
            dma((3, 7)),
            dma((3, 7)),
            dma((2, 8)),
            dma((2, 8)),
            dma((5, 8)),
            dma((5, 8)),
        ],
        compiler_params=pltpu.CompilerParams(
            collective_id=1, has_side_effects=True, vmem_limit_bytes=60 * 2**20
        ),
    )(
        video,
        text,
        w_qkv,
        w_out.reshape(3, 128, WIDTH),
        shift.reshape(1, -1),
        scale.reshape(1, -1),
        gate.reshape(1, -1),
        q_gain.reshape(1, HD),
        k_gain.reshape(1, HD),
        jnp.asarray(freqs),
        clip_lengths,
        text_owner,
    )


def solution(mesh):
    return jax.shard_map(
        on_device,
        mesh=mesh,
        in_specs=(
            P(("dp", "blk"), "head"),
            P(("dp", "blk"), "head"),
            P(),
            P(),
            P(),
            P("blk", "head"),
            P("head", "blk"),
            P(),
            P(),
            P("dp"),
            P("dp"),
        ),
        out_specs=(P(("dp", "blk"), "head"), P(("dp", "blk"), "head")),
        check_vma=False,
    )
```

```python
import functools
import math

import jax
import jax.numpy as jnp
import numpy as np
from jax import lax
from jax.experimental import pallas as pl
from jax.experimental.pallas import tpu as pltpu
from jax.sharding import PartitionSpec as P

MESH = pl.DeviceIdType.MESH
BF = jnp.bfloat16
F32 = jnp.float32
ROWS = 640
VROWS = 512
WIDTH = 384
HD = 128
TILE = 128


def remote(src, dst, send_sem, recv_sem, device):
    return pltpu.make_async_remote_copy(
        src_ref=src,
        dst_ref=dst,
        send_sem=send_sem,
        recv_sem=recv_sem,
        device_id=device,
        device_id_type=MESH,
    )


def greet(devices):
    barrier = pltpu.get_barrier_semaphore()
    for device in devices:
        pl.semaphore_signal(barrier, inc=1, device_id=device, device_id_type=MESH)
    pl.semaphore_wait(barrier, len(devices))


PARTS = {
    "all": (0, 128, 0),
    "f0": (0, 64, 0),
    "f1": (64, 64, 1),
    "a": (0, 96, 0),
    "b": (96, 32, 1),
    "a0": (0, 48, 0),
    "a1": (48, 48, 2),
}


def sublayer_kernel(
    video,
    text,
    w_qkv,
    w_out,
    shift_in,
    scale_in,
    gate_in,
    q_gain_in,
    k_gain_in,
    freqs_in,
    lengths,
    owners,
    video_out,
    text_out,
    tok,
    mod,
    wkv,
    wq,
    ring,
    wo,
    cos_t,
    sin_t,
    shift,
    scale,
    gate,
    q_gain,
    k_gain,
    freqs,
    q_block,
    q,
    kvbuf,
    att,
    proj,
    best,
    total,
    acc,
    q_clip,
    local_sem,
    tok_recv,
    tok_send,
    wl_recv,
    wr_recv,
    wr_send,
    wl_send,
    sib_recv,
    sib_send,
    q_recv,
    q_send,
    ol_recv,
    or_recv,
    or_send,
    ol_send,
    swap_recv,
    swap_send,
    share_recv,
    share_send,
    left_recv,
    right_recv,
    right_send,
    left_send,
    att_recv,
    att_send,
    last_recv,
    last_send,
):
    dp, z, head = lax.axis_index("dp"), lax.axis_index("blk"), lax.axis_index("head")
    core = lax.rem(dp, 2)
    yh, x = head // 4, lax.rem(head, 4)
    sibling = (dp + 1 - 2 * core, z, head)
    mates = [sibling] + [
        (d, z, head) for d in (lax.rem(dp + 2, 4), lax.rem(dp + 2, 4) + 1 - 2 * core)
    ]
    up, down = (dp, lax.rem(z + 1, 8), head), (dp, lax.rem(z + 7, 8), head)
    xs = [lax.rem(x + d, 4) for d in range(4)]
    slot = [[yh * 4 + xs[d] for d in range(4)], [(1 - yh) * 4 + xs[d] for d in range(4)]]
    right, left, over = (dp, z, slot[0][1]), (dp, z, slot[0][3]), (dp, z, slot[1][0])
    peers = [(dp, z, lax.rem(head + d, 8)) for d in range(1, 8)]
    greet(peers + [up, down] + mates)

    sends = []

    def send(copy):
        copy.start()
        sends.append(copy)

    def landed(ref, sem):
        pltpu.make_async_copy(ref, ref, sem).wait()

    def cols_of(h):
        return pl.ds(pl.multiple_of(h * WIDTH, WIDTH), WIDTH)

    def tok_at(h, t, part):
        first, count, _ = PARTS[part]
        return tok.at[pl.ds(t * TILE + first, count), cols_of(h)]

    def own_tile(t):
        return video.at[pl.ds(t * TILE, TILE)] if t < 4 else text.at[pl.ds(0, TILE)]

    send_count = [0]

    def tok_copy(src, h, t, part, flip, dx, device):
        index = send_count[0]
        send_count[0] += 1
        arrival = tok_recv.at[flip, dx, t, PARTS[part][2]]
        send(remote(src, tok_at(h, t, part), tok_send.at[index], arrival, device))

    def tok_pass(h, t, part, flip, dx, device):
        tok_copy(tok_at(h, t, part), h, t, part, flip, dx, device)

    def tok_wait(flip, dx, t, part):
        landed(tok_at(slot[flip][dx], t, part), tok_recv.at[flip, dx, t, PARTS[part][2]])

    def stage0(t):
        tok_copy(own_tile(t), head, t, "all", 0, 3, right)
        tok_copy(own_tile(t), head, t, "all", 0, 1, left)
        tok_copy(own_tile(t), head, t, "all", 1, 0, over)

    def stage1(t):
        tok_wait(1, 0, t, "all")
        tok_pass(slot[1][0], t, "a", 1, 3, right)
        tok_pass(slot[1][0], t, "a", 1, 1, left)
        for dx, part, device in ((3, "f0", right), (1, "f1", left)):
            tok_wait(0, dx, t, "all")
            tok_pass(slot[0][dx], t, part, 0, 2, device)
            tok_pass(slot[0][dx], t, "b", 1, dx, over)

    def stage2(t):
        for dx, part, device in ((3, "a0", right), (1, "a1", left)):
            tok_wait(1, dx, t, "a")
            tok_pass(slot[1][dx], t, part, 1, 2, device)
        tok_wait(0, 2, t, "f0")
        tok_wait(0, 2, t, "f1")
        tok_pass(slot[0][2], t, "b", 1, 2, over)

    def stage3(t):
        for dx, part in ((2, "a0"), (2, "a1"), (1, "b"), (3, "b"), (2, "b")):
            tok_wait(1, dx, t, part)
        normalise(t)

    def normalise(t):
        @pl.loop(0, 8, unroll=4)
        def _(i):
            rows = pl.ds(pl.multiple_of(t * TILE + i * 16, 16), 16)
            value = tok[rows, :].astype(F32)
            mean = jnp.sum(value, axis=1, keepdims=True) * (1.0 / 3072.0)
            value = value - mean
            var = jnp.sum(value * value, axis=1, keepdims=True) * (1.0 / 3072.0)
            value = value * lax.rsqrt(var + 1e-06) * (1.0 + scale[...]) + shift[...]
            mod[rows, :] = value.astype(BF)

    def w_at(block, p, half=None, side=None):
        first, count = (0, 192) if half is None else (half * 96, 96)
        side = core if side is None else side
        rows = pl.ds(pl.multiple_of(block * WIDTH + side * 192 + first, 32), count)
        return wkv.at[rows, pl.ds(256 * p, 256)]

    def w_cols(p):
        return pl.ds(384 * p + 128, 256) if p < 3 else pl.ds(384 * (p - 3), 128)

    def ring_first(p):
        src = w_qkv.at[pl.ds(pl.multiple_of(core * 192, 192), 192), w_cols(p)]
        send(remote(src, w_at(z, p), wr_send.at[p, 0], wl_recv.at[p, 0], up))
        send(remote(src, w_at(z, p), wl_send.at[p, 0], wr_recv.at[p, 0], down))

    def ring_step(p, s):
        lo, hi = lax.rem(z + 8 - s, 8), lax.rem(z + s, 8)
        half_a, half_b = (0, 1) if s == 4 else (None, None)
        landed(w_at(lo, p, half_a), wl_recv.at[p, s - 1])
        if s < 4:
            src = w_at(lo, p, 0 if s == 3 else None)
            send(remote(src, src, wr_send.at[p, s], wl_recv.at[p, s], up))
        landed(w_at(hi, p, half_b), wr_recv.at[p, s - 1])
        if s < 4:
            src = w_at(hi, p, 1 if s == 3 else None)
            send(remote(src, src, wl_send.at[p, s], wr_recv.at[p, s], down))
        for i, (block, half) in enumerate(((lo, half_a), (hi, half_b))):
            ref = w_at(block, p, half)
            k = 2 * (s - 1) + i
            send(remote(ref, ref, sib_send.at[p, k], sib_recv.at[p, k], sibling))

    def sib_wait(p):
        for s in range(1, 5):
            for i in range(2):
                block = lax.rem(z + 8 - s, 8) if i == 0 else lax.rem(z + s, 8)
                ref = w_at(block, p, i if s == 4 else None, 1 - core)
                landed(ref, sib_recv.at[p, 2 * (s - 1) + i])

    def q_at(block, half, quarter):
        part = wq.at[block, quarter]
        return part if half is None else part.at[pl.ds(half * 48, 48)]

    def q_pair(s, quarter, split):
        lo, hi = lax.rem(z + 8 - s, 8), lax.rem(z + s, 8)
        return q_at(lo, 0 if split else None, quarter), q_at(hi, 1 if split else None, quarter)

    def q_sends(s):
        a, b = q_pair(s, dp, s == 3)
        send(remote(a, a, wr_send.at[3, s], wl_recv.at[3, s], up))
        send(remote(b, b, wl_send.at[3, s], wr_recv.at[3, s], down))

    def q_step(s):
        a, b = q_pair(s, dp, s == 4)
        landed(a, wl_recv.at[3, s - 1])
        landed(b, wr_recv.at[3, s - 1])
        if s < 4:
            q_sends(s)
        for i in range(2):
            for k, ref in enumerate((a, b)):
                n = 2 * (s - 1) + k
                send(remote(ref, ref, q_send.at[i, n], q_recv.at[i, n], mates[i]))

    def q_on():
        for s in range(1, 5):
            for k, ref in enumerate(q_pair(s, mates[1][0], s == 4)):
                landed(ref, q_recv.at[1, 2 * (s - 1) + k])
        part = wq.at[:, mates[1][0]]
        send(remote(part, part, q_send.at[2, 0], q_recv.at[2, 0], sibling))

    def q_wait():
        for s in range(1, 5):
            for k, ref in enumerate(q_pair(s, sibling[0], s == 4)):
                landed(ref, q_recv.at[0, 2 * (s - 1) + k])
        landed(wq.at[:, mates[2][0]], q_recv.at[2, 0])

    quarter = w_out.at[:, pl.ds(pl.multiple_of(dp * 32, 32), 32)]

    def out_first():
        send(remote(quarter, ring.at[z], or_send.at[0], ol_recv.at[0], up))
        send(remote(quarter, ring.at[z], ol_send.at[0], or_recv.at[0], down))

    def out_at(block, half):
        return ring.at[block] if half is None else ring.at[block, :, pl.ds(half * 16, 16)]

    def out_sends(s):
        lo, hi = lax.rem(z + 8 - s, 8), lax.rem(z + s, 8)
        a, b = out_at(lo, 0 if s == 3 else None), out_at(hi, 1 if s == 3 else None)
        return (
            remote(a, a, or_send.at[s], ol_recv.at[s], up),
            remote(b, b, ol_send.at[s], or_recv.at[s], down),
        )

    def out_step(s):
        lo, hi = lax.rem(z + 8 - s, 8), lax.rem(z + s, 8)
        landed(out_at(lo, 0 if s == 4 else None), ol_recv.at[s - 1])
        landed(out_at(hi, 1 if s == 4 else None), or_recv.at[s - 1])
        if s < 4:
            for copy in out_sends(s):
                send(copy)

    def swap_copy(d):
        block = lax.rem(head + d, 8)
        target = wo.at[:, head, dp]
        return remote(
            ring.at[block], target, swap_send.at[d], swap_recv.at[8 - d], (dp, z, block)
        )

    swap_own = pltpu.make_async_copy(ring.at[head], wo.at[:, head, dp], swap_recv.at[0])

    def swap():
        for d in range(1, 8):
            swap_copy(d).start()
        swap_own.start()

    def share_copy(i):
        part = wo.at[:, :, mates[1][0] if i == 2 else dp]
        return remote(part, part, share_send.at[i], share_recv.at[i], mates[i % 2])

    def share():
        for d in range(8):
            landed(wo.at[:, lax.rem(head + d, 8), dp], swap_recv.at[d])
        for i in range(2):
            share_copy(i).start()

    def share_on():
        landed(wo.at[:, :, mates[1][0]], share_recv.at[1])
        share_copy(2).start()

    def share_wait():
        landed(wo.at[:, :, mates[0][0]], share_recv.at[0])
        landed(wo.at[:, :, mates[2][0]], share_recv.at[2])

    own = [
        pltpu.make_async_copy(video, tok.at[pl.ds(0, VROWS), cols_of(head)], local_sem.at[0]),
        pltpu.make_async_copy(
            text, tok.at[pl.ds(VROWS, ROWS - VROWS), cols_of(head)], local_sem.at[1]
        ),
        pltpu.make_async_copy(quarter, ring.at[z], local_sem.at[2]),
    ]
    block_rows = pl.ds(pl.multiple_of(z * WIDTH, WIDTH), WIDTH)
    own_queries, own_quarters = [], []
    for p in range(3):
        own.append(
            pltpu.make_async_copy(
                w_qkv.at[:, w_cols(p)],
                wkv.at[block_rows, pl.ds(256 * p, 256)],
                local_sem.at[3 + p],
            )
        )
        own_queries.append(
            pltpu.make_async_copy(
                w_qkv.at[:, w_cols(3 + p)],
                q_block.at[:, pl.ds(128 * p, 128)],
                local_sem.at[6 + p],
            )
        )
    for i, quarter_of in enumerate((dp, mates[0][0], mates[1][0])):
        rows = pl.ds(pl.multiple_of(quarter_of * 96, 96), 96)
        own_quarters.append(
            pltpu.make_async_copy(q_block.at[rows], wq.at[z, quarter_of], local_sem.at[15 + i])
        )
    small = [
        pltpu.make_async_copy(a, b, local_sem.at[9 + i])
        for i, (a, b) in enumerate(
            (
                (freqs_in, freqs),
                (shift_in, shift),
                (scale_in, scale),
                (q_gain_in, q_gain),
                (k_gain_in, k_gain),
                (gate_in.at[:, cols_of(head)], gate),
            )
        )
    ]
    for copy in own_queries:
        copy.start()
    for p in range(3):
        ring_first(p)
    for t in range(5):
        stage0(t)
    for copy in small + own:
        copy.start()
    for copy in small:
        copy.wait()

    def query_first():
        src = q_block.at[pl.ds(pl.multiple_of(dp * 96, 96), 96)]
        send(remote(src, wq.at[z, dp], wr_send.at[3, 0], wl_recv.at[3, 0], up))
        send(remote(src, wq.at[z, dp], wl_send.at[3, 0], wr_recv.at[3, 0], down))

    e0 = lengths[0]
    e1 = e0 + lengths[1]
    e2 = e1 + lengths[2]

    def clips(place, is_video, owner):
        ids = (
            (place >= e0).astype(jnp.int32)
            + (place >= e1).astype(jnp.int32)
            + (place >= e2).astype(jnp.int32)
        )
        return jnp.where(is_video, ids, owner)

    def tables(t):
        rows = pl.ds(t * TILE, TILE)
        row = lax.broadcasted_iota(jnp.int32, (TILE, HD), 0) + t * TILE
        place = z * VROWS + row
        q_clip[rows, :] = clips(place, row < VROWS, owners[z // 2])
        start = jnp.where(place >= e0, e0, 0)
        start = jnp.where(place >= e1, e1, start)
        start = jnp.where(place >= e2, e2, start)
        place = jnp.where(row < VROWS, place - start, 0).astype(F32)
        angle = place * freqs[...]
        lane = lax.broadcasted_iota(jnp.int32, (TILE, HD), 1)
        sine = jnp.sin(angle)
        cos_t[rows, :] = jnp.cos(angle)
        sin_t[rows, :] = jnp.where(lane < HD // 2, -sine, sine)

    def rms_rope(value, gain):
        mean = jnp.sum(value * value, axis=1, keepdims=True) * (1.0 / HD)
        value = value * lax.rsqrt(mean + 1e-06) * gain
        return value * cos_t[...] + pltpu.roll(value, HD // 2, 1) * sin_t[...]

    def ring_steps(s, *pieces):
        for p in pieces:
            if p == 4:
                out_step(s)
            elif p == 3:
                q_step(s)
            else:
                ring_step(p, s)

    for t in range(5):
        tables(t)
        stage1(t)
        if t < 3:
            ring_steps(1, t)
    for copy in own_queries:
        copy.wait()
    for copy in own_quarters:
        copy.start()
    query_first()
    out_first()
    for t in range(5):
        stage2(t)
        if t < 3:
            ring_steps(2, t)
    for copy in own + own_quarters:
        copy.wait()
    ring_steps(1, 3, 4)
    stage3(0)
    ring_steps(3, 0, 1, 2)
    stage3(1)
    ring_steps(2, 3, 4)
    stage3(2)
    ring_steps(4, 0, 1, 2)
    ring_steps(3, 3, 4)
    stage3(3)
    stage3(4)
    sib_wait(0)

    def own_sends(h):
        for i in range(2):
            a, b = kvbuf.at[h, z, i], kvbuf.at[h, z, 1 - i]
            remote(a, a, right_send.at[h, i], left_recv.at[h, i], up).start()
            remote(b, b, left_send.at[h, i], right_recv.at[h, i], down).start()

    def pass_on(h, j):
        odd = lax.rem(j, 2)
        lo, hi = lax.rem(z + 7 - j // 2, 8), lax.rem(z + 1 + j // 2, 8)
        from_left, from_right = kvbuf.at[h, lo, odd], kvbuf.at[h, hi, 1 - odd]
        landed(from_left, left_recv.at[h, j])

        @pl.when(j < 5)
        def _():
            remote(
                from_left, from_left, right_send.at[h, j + 2], left_recv.at[h, j + 2], up
            ).start()

        landed(from_right, right_recv.at[h, j])

        @pl.when(j < 5)
        def _():
            remote(
                from_right, from_right, left_send.at[h, j + 2], right_recv.at[h, j + 2], down
            ).start()

    for h in range(3):
        kv = jnp.dot(mod[...], wkv[:, 256 * h : 256 * h + 256], preferred_element_type=F32)
        keys = rms_rope(kv[:, 0:HD], k_gain[...]).astype(BF)
        values = kv[:, HD : 2 * HD].astype(BF)
        for i in range(2):
            rows = slice(i * (ROWS // 2), (i + 1) * (ROWS // 2))
            kvbuf[h, z, i, :, 0:HD] = keys[rows]
            kvbuf[h, z, i, :, HD : 2 * HD] = values[rows]
        if h == 0:
            own_sends(0)
            ring_steps(4, 3, 4)
            q_on()
            swap()
            sib_wait(1)
            sib_wait(2)
        elif h == 1:
            own_sends(1)
            pass_on(0, 0)
    q_wait()
    pass_on(0, 1)
    queries = jnp.dot(mod[...], wq[...].reshape(3072, WIDTH), preferred_element_type=F32)
    for h in range(3):
        q[h] = rms_rope(queries[:, h * HD : (h + 1) * HD], q_gain[...]).astype(BF)
    proj[...] = jnp.zeros_like(proj)

    factor = math.log2(math.e) / math.sqrt(HD)
    mine = pl.ds(pl.multiple_of(head * HD, HD), HD)

    def unit(h, b, first, each=None):
        keys = kvbuf[h, b, :, :, 0:HD].reshape(ROWS, HD)
        values = kvbuf[h, b, :, :, HD : 2 * HD].reshape(ROWS, HD)
        column = lax.broadcasted_iota(jnp.int32, (1, ROWS), 1)
        key_clip = clips(b * VROWS + column, column < VROWS, owners[b // 2])
        tiles = [pl.ds(t * TILE, TILE) for t in range(5)]
        scored = [
            lax.dot_general(
                q[h, rows, :], keys, (((1,), (1,)), ((), ())), preferred_element_type=F32
            )
            for rows in tiles
        ]
        weighed = []
        for rows, scores in zip(tiles, scored):
            scores = jnp.where(q_clip[rows, 0:1] == key_clip, scores, -1e30)
            old = jnp.where(first, -1e30, best[rows, 0:1])
            newest = jnp.maximum(old, jnp.max(scores, axis=1, keepdims=True))
            weights = jnp.exp2((scores - newest) * factor)
            best[rows, :] = jnp.broadcast_to(newest, (TILE, HD))
            weighed.append((weights, jnp.exp2((old - newest) * factor)))
        for t, (rows, (weights, keep)) in enumerate(zip(tiles, weighed)):
            count = jnp.sum(weights, axis=1, keepdims=True)
            summed = jnp.dot(weights.astype(BF), values, preferred_element_type=F32)
            prior = jnp.where(first, 0.0, total[rows, 0:1])
            before = jnp.where(first, 0.0, acc[rows, :])
            total[rows, :] = jnp.broadcast_to(prior * keep + count, (TILE, HD))
            acc[rows, :] = before * keep + summed
            if each is not None:
                each(t)

    def att_copy(h, d):
        part = att.at[h, :, mine]
        return remote(part, part, att_send.at[h, d], att_recv.at[h, 8 - d], peers[d - 1])

    def finish(h):
        att[h, :, mine] = (acc[...] / total[...]).astype(BF)
        for d in range(1, 8):
            att_copy(h, d).start()

    def from_peer(d):
        return pl.ds(pl.multiple_of(lax.rem(head + d, 8) * HD, HD), HD)

    def out_project(h):
        for d in range(1, 8):
            landed(att.at[h, :, from_peer(d)], att_recv.at[h, d])
        proj[...] += jnp.dot(att[h], wo[h].reshape(8 * HD, WIDTH), preferred_element_type=F32)

    def last_copy(t, d):
        part = att.at[2, pl.ds(t * TILE, TILE), mine]
        return remote(part, part, last_send.at[t, d], last_recv.at[t, 8 - d], peers[d - 1])

    def finish_tile(t):
        rows = pl.ds(t * TILE, TILE)
        att[2, rows, mine] = (acc[rows, :] / total[rows, :]).astype(BF)
        for d in range(1, 8):
            last_copy(t, d).start()

    def step(t, carry):
        h, j = t // 7, lax.rem(t, 7)
        odd = lax.rem(j, 2)

        @pl.when(t >= 2)
        def _():
            pass_on(h, j)

        @pl.when(t == 4)
        def _():
            own_sends(2)

        @pl.when(t == 1)
        def _():
            share()

        @pl.when(t == 8)
        def _():
            share_on()

        away = jnp.where(j == 6, 4, (j + 1) // 2)
        unit(h, lax.rem(jnp.where(odd == 1, z + 8 - away, z + away), 8), j == 0)

        @pl.when(j == 5)
        def _():
            unit(h, lax.rem(z + 3, 8), False)

        @pl.when(j == 6)
        def _():
            finish(h)

        @pl.when(t == 17)
        def _():
            share_wait()
            out_project(0)

        @pl.when(t == 19)
        def _():
            out_project(1)

        return carry

    lax.fori_loop(0, 20, step, 0)
    pass_on(2, 6)
    unit(2, lax.rem(z + 4, 8), False, finish_tile)
    weights_out = wo[2].reshape(8 * HD, WIDTH)
    for t in range(5):
        rows = pl.ds(t * TILE, TILE)
        for d in range(1, 8):
            landed(att.at[2, rows, from_peer(d)], last_recv.at[t, d])
        summed = proj[rows, :] + jnp.dot(att[2, rows, :], weights_out, preferred_element_type=F32)
        residual = tok[rows, cols_of(head)].astype(F32)
        result = (residual + gate[...] * summed).astype(BF)
        if t < 4:
            video_out[rows, :] = result
        else:
            text_out[...] = result

    def drain(t, carry):
        h, j = t // 7, lax.rem(t, 7)
        part = kvbuf.at[h, z, 0]
        remote(part, part, right_send.at[h, j], left_recv.at[h, j], up).wait_send()
        remote(part, part, left_send.at[h, j], right_recv.at[h, j], down).wait_send()
        return carry

    lax.fori_loop(0, 21, drain, 0)
    for d in range(1, 8):
        swap_copy(d).wait_send()
        for h in range(2):
            att_copy(h, d).wait_send()
        for t in range(5):
            last_copy(t, d).wait_send()
    for i in range(3):
        share_copy(i).wait_send()
    for copy in sends:
        copy.wait_send()


def on_device(
    video, text, shift, scale, gate, w_qkv, w_out, q_gain, k_gain, clip_lengths, text_owner
):
    anywhere = pl.BlockSpec(memory_space=pl.ANY)
    vmem = pl.BlockSpec(memory_space=pltpu.VMEM)
    smem = pl.BlockSpec(memory_space=pltpu.SMEM)
    dma = pltpu.SemaphoreType.DMA
    exponents = np.arange(HD // 2, dtype=np.float64) * (-2.0 / HD)
    freqs = np.tile((10000.0**exponents).astype(np.float32), 2).reshape(1, HD)
    return pl.pallas_call(
        sublayer_kernel,
        name="sublayer",
        out_shape=(
            jax.ShapeDtypeStruct((VROWS, WIDTH), BF),
            jax.ShapeDtypeStruct((ROWS - VROWS, WIDTH), BF),
        ),
        in_specs=[anywhere] * 10 + [smem] * 2,
        out_specs=(vmem, vmem),
        scratch_shapes=[
            pltpu.VMEM((ROWS, 3072), BF),
            pltpu.VMEM((ROWS, 3072), BF),
            pltpu.VMEM((3072, 768), BF),
            pltpu.VMEM((8, 4, 96, WIDTH), BF),
            pltpu.VMEM((8, 3, 32, WIDTH), BF),
            pltpu.VMEM((3, 8, 4, 32, WIDTH), BF),
            pltpu.VMEM((ROWS, HD), F32),
            pltpu.VMEM((ROWS, HD), F32),
            pltpu.VMEM((1, 3072), F32),
            pltpu.VMEM((1, 3072), F32),
            pltpu.VMEM((1, WIDTH), F32),
            pltpu.VMEM((1, HD), F32),
            pltpu.VMEM((1, HD), F32),
            pltpu.VMEM((1, HD), F32),
            pltpu.VMEM((WIDTH, WIDTH), BF),
            pltpu.VMEM((3, ROWS, HD), BF),
            pltpu.VMEM((3, 8, 2, ROWS // 2, 2 * HD), BF),
            pltpu.VMEM((3, ROWS, 8 * HD), BF),
            pltpu.VMEM((ROWS, WIDTH), F32),
            pltpu.VMEM((ROWS, HD), F32),
            pltpu.VMEM((ROWS, HD), F32),
            pltpu.VMEM((ROWS, HD), F32),
            pltpu.VMEM((ROWS, HD), jnp.int32),
            dma((18,)),
            dma((2, 4, 5, 3)),
            dma((64,)),
            dma((4, 4)),
            dma((4, 4)),
            dma((4, 4)),
            dma((4, 4)),
            dma((3, 8)),
            dma((3, 8)),
            dma((3, 8)),
            dma((3, 8)),
            dma((4,)),
            dma((4,)),
            dma((4,)),
            dma((4,)),
            dma((8,)),
            dma((8,)),
            dma((3,)),
            dma((3,)),
            dma((3, 7)),
            dma((3, 7)),
            dma((3, 7)),
            dma((3, 7)),
            dma((2, 8)),
            dma((2, 8)),
            dma((5, 8)),
            dma((5, 8)),
        ],
        compiler_params=pltpu.CompilerParams(
            collective_id=1, has_side_effects=True, vmem_limit_bytes=60 * 2**20
        ),
    )(
        video,
        text,
        w_qkv,
        w_out.reshape(3, 128, WIDTH),
        shift.reshape(1, -1),
        scale.reshape(1, -1),
        gate.reshape(1, -1),
        q_gain.reshape(1, HD),
        k_gain.reshape(1, HD),
        jnp.asarray(freqs),
        clip_lengths,
        text_owner,
    )


def solution(mesh):
    return jax.shard_map(
        on_device,
        mesh=mesh,
        in_specs=(
            P(("dp", "blk"), "head"),
            P(("dp", "blk"), "head"),
            P(),
            P(),
            P(),
            P("blk", "head"),
            P("head", "blk"),
            P(),
            P(),
            P("dp"),
            P("dp"),
        ),
        out_specs=(P(("dp", "blk"), "head"), P(("dp", "blk"), "head")),
        check_vma=False,
    )
```

```python
import functools
import math

import jax
import jax.numpy as jnp
import numpy as np
from jax import lax
from jax.experimental import pallas as pl
from jax.experimental.pallas import tpu as pltpu
from jax.sharding import PartitionSpec as P

MESH = pl.DeviceIdType.MESH
BF = jnp.bfloat16
F32 = jnp.float32
ROWS = 640
VROWS = 512
WIDTH = 384
HD = 128
TILE = 128


def remote(src, dst, send_sem, recv_sem, device):
    return pltpu.make_async_remote_copy(
        src_ref=src,
        dst_ref=dst,
        send_sem=send_sem,
        recv_sem=recv_sem,
        device_id=device,
        device_id_type=MESH,
    )


def greet(devices):
    barrier = pltpu.get_barrier_semaphore()
    for device in devices:
        pl.semaphore_signal(barrier, inc=1, device_id=device, device_id_type=MESH)
    pl.semaphore_wait(barrier, len(devices))


PARTS = {
    "all": (0, 128, 0),
    "f0": (0, 64, 0),
    "f1": (64, 64, 1),
    "a": (0, 80, 0),
    "b": (80, 48, 1),
    "a0": (0, 48, 0),
    "a1": (48, 32, 2),
}


def sublayer_kernel(
    video,
    text,
    w_qkv,
    w_out,
    shift_in,
    scale_in,
    gate_in,
    q_gain_in,
    k_gain_in,
    freqs_in,
    lengths,
    owners,
    video_out,
    text_out,
    tok,
    mod,
    wkv,
    wq,
    ring,
    wo,
    cos_t,
    sin_t,
    shift,
    scale,
    gate,
    q_gain,
    k_gain,
    freqs,
    q_block,
    q,
    kvbuf,
    att,
    proj,
    best,
    total,
    acc,
    q_clip,
    local_sem,
    tok_recv,
    tok_send,
    wl_recv,
    wr_recv,
    wr_send,
    wl_send,
    sib_recv,
    sib_send,
    q_recv,
    q_send,
    ol_recv,
    or_recv,
    or_send,
    ol_send,
    swap_recv,
    swap_send,
    share_recv,
    share_send,
    left_recv,
    right_recv,
    right_send,
    left_send,
    att_recv,
    att_send,
    last_recv,
    last_send,
):
    dp, z, head = lax.axis_index("dp"), lax.axis_index("blk"), lax.axis_index("head")
    core = lax.rem(dp, 2)
    yh, x = head // 4, lax.rem(head, 4)
    sibling = (dp + 1 - 2 * core, z, head)
    mates = [sibling] + [
        (d, z, head) for d in (lax.rem(dp + 2, 4), lax.rem(dp + 2, 4) + 1 - 2 * core)
    ]
    up, down = (dp, lax.rem(z + 1, 8), head), (dp, lax.rem(z + 7, 8), head)
    xs = [lax.rem(x + d, 4) for d in range(4)]
    slot = [[yh * 4 + xs[d] for d in range(4)], [(1 - yh) * 4 + xs[d] for d in range(4)]]
    right, left, over = (dp, z, slot[0][1]), (dp, z, slot[0][3]), (dp, z, slot[1][0])
    peers = [(dp, z, lax.rem(head + d, 8)) for d in range(1, 8)]
    greet(peers + [up, down] + mates)

    sends = []

    def send(copy):
        copy.start()
        sends.append(copy)

    def landed(ref, sem):
        pltpu.make_async_copy(ref, ref, sem).wait()

    def cols_of(h):
        return pl.ds(pl.multiple_of(h * WIDTH, WIDTH), WIDTH)

    def tok_at(h, t, part):
        first, count, _ = PARTS[part]
        return tok.at[pl.ds(t * TILE + first, count), cols_of(h)]

    def own_tile(t):
        return video.at[pl.ds(t * TILE, TILE)] if t < 4 else text.at[pl.ds(0, TILE)]

    send_count = [0]

    def tok_copy(src, h, t, part, flip, dx, device):
        index = send_count[0]
        send_count[0] += 1
        arrival = tok_recv.at[flip, dx, t, PARTS[part][2]]
        send(remote(src, tok_at(h, t, part), tok_send.at[index], arrival, device))

    def tok_pass(h, t, part, flip, dx, device):
        tok_copy(tok_at(h, t, part), h, t, part, flip, dx, device)

    def tok_wait(flip, dx, t, part):
        landed(tok_at(slot[flip][dx], t, part), tok_recv.at[flip, dx, t, PARTS[part][2]])

    def stage0(t):
        tok_copy(own_tile(t), head, t, "all", 0, 3, right)
        tok_copy(own_tile(t), head, t, "all", 0, 1, left)
        tok_copy(own_tile(t), head, t, "all", 1, 0, over)

    def stage1(t):
        tok_wait(1, 0, t, "all")
        tok_pass(slot[1][0], t, "a", 1, 3, right)
        tok_pass(slot[1][0], t, "a", 1, 1, left)
        for dx, part, device in ((3, "f0", right), (1, "f1", left)):
            tok_wait(0, dx, t, "all")
            tok_pass(slot[0][dx], t, part, 0, 2, device)
            tok_pass(slot[0][dx], t, "b", 1, dx, over)

    def stage2(t):
        for dx, part, device in ((3, "a0", right), (1, "a1", left)):
            tok_wait(1, dx, t, "a")
            tok_pass(slot[1][dx], t, part, 1, 2, device)
        tok_wait(0, 2, t, "f0")
        tok_wait(0, 2, t, "f1")
        tok_pass(slot[0][2], t, "b", 1, 2, over)

    def stage3(t):
        for dx, part in ((2, "a0"), (2, "a1"), (1, "b"), (3, "b"), (2, "b")):
            tok_wait(1, dx, t, part)
        normalise(t)

    def normalise(t):
        @pl.loop(0, 8, unroll=4)
        def _(i):
            rows = pl.ds(pl.multiple_of(t * TILE + i * 16, 16), 16)
            value = tok[rows, :].astype(F32)
            mean = jnp.sum(value, axis=1, keepdims=True) * (1.0 / 3072.0)
            value = value - mean
            var = jnp.sum(value * value, axis=1, keepdims=True) * (1.0 / 3072.0)
            value = value * lax.rsqrt(var + 1e-06) * (1.0 + scale[...]) + shift[...]
            mod[rows, :] = value.astype(BF)

    def w_at(block, p, half=None, side=None):
        first, count = (0, 192) if half is None else (half * 96, 96)
        side = core if side is None else side
        rows = pl.ds(pl.multiple_of(block * WIDTH + side * 192 + first, 32), count)
        return wkv.at[rows, pl.ds(256 * p, 256)]

    def w_cols(p):
        return pl.ds(384 * p + 128, 256) if p < 3 else pl.ds(384 * (p - 3), 128)

    def ring_first(p):
        src = w_qkv.at[pl.ds(pl.multiple_of(core * 192, 192), 192), w_cols(p)]
        send(remote(src, w_at(z, p), wr_send.at[p, 0], wl_recv.at[p, 0], up))
        send(remote(src, w_at(z, p), wl_send.at[p, 0], wr_recv.at[p, 0], down))

    def ring_step(p, s):
        lo, hi = lax.rem(z + 8 - s, 8), lax.rem(z + s, 8)
        half_a, half_b = (0, 1) if s == 4 else (None, None)
        landed(w_at(lo, p, half_a), wl_recv.at[p, s - 1])
        if s < 4:
            src = w_at(lo, p, 0 if s == 3 else None)
            send(remote(src, src, wr_send.at[p, s], wl_recv.at[p, s], up))
        landed(w_at(hi, p, half_b), wr_recv.at[p, s - 1])
        if s < 4:
            src = w_at(hi, p, 1 if s == 3 else None)
            send(remote(src, src, wl_send.at[p, s], wr_recv.at[p, s], down))
        for i, (block, half) in enumerate(((lo, half_a), (hi, half_b))):
            ref = w_at(block, p, half)
            k = 2 * (s - 1) + i
            send(remote(ref, ref, sib_send.at[p, k], sib_recv.at[p, k], sibling))

    def sib_wait(p):
        for s in range(1, 5):
            for i in range(2):
                block = lax.rem(z + 8 - s, 8) if i == 0 else lax.rem(z + s, 8)
                ref = w_at(block, p, i if s == 4 else None, 1 - core)
                landed(ref, sib_recv.at[p, 2 * (s - 1) + i])

    def q_at(block, half, quarter):
        part = wq.at[block, quarter]
        return part if half is None else part.at[pl.ds(half * 48, 48)]

    def q_pair(s, quarter, split):
        lo, hi = lax.rem(z + 8 - s, 8), lax.rem(z + s, 8)
        return q_at(lo, 0 if split else None, quarter), q_at(hi, 1 if split else None, quarter)

    def q_sends(s):
        a, b = q_pair(s, dp, s == 3)
        send(remote(a, a, wr_send.at[3, s], wl_recv.at[3, s], up))
        send(remote(b, b, wl_send.at[3, s], wr_recv.at[3, s], down))

    def q_step(s):
        a, b = q_pair(s, dp, s == 4)
        landed(a, wl_recv.at[3, s - 1])
        landed(b, wr_recv.at[3, s - 1])
        if s < 4:
            q_sends(s)
        for i in range(2):
            for k, ref in enumerate((a, b)):
                n = 2 * (s - 1) + k
                send(remote(ref, ref, q_send.at[i, n], q_recv.at[i, n], mates[i]))

    def q_on():
        for s in range(1, 5):
            for k, ref in enumerate(q_pair(s, mates[1][0], s == 4)):
                landed(ref, q_recv.at[1, 2 * (s - 1) + k])
        part = wq.at[:, mates[1][0]]
        send(remote(part, part, q_send.at[2, 0], q_recv.at[2, 0], sibling))

    def q_wait():
        for s in range(1, 5):
            for k, ref in enumerate(q_pair(s, sibling[0], s == 4)):
                landed(ref, q_recv.at[0, 2 * (s - 1) + k])
        landed(wq.at[:, mates[2][0]], q_recv.at[2, 0])

    quarter = w_out.at[:, pl.ds(pl.multiple_of(dp * 32, 32), 32)]

    def out_first():
        send(remote(quarter, ring.at[z], or_send.at[0], ol_recv.at[0], up))
        send(remote(quarter, ring.at[z], ol_send.at[0], or_recv.at[0], down))

    def out_at(block, half):
        return ring.at[block] if half is None else ring.at[block, :, pl.ds(half * 16, 16)]

    def out_sends(s):
        lo, hi = lax.rem(z + 8 - s, 8), lax.rem(z + s, 8)
        a, b = out_at(lo, 0 if s == 3 else None), out_at(hi, 1 if s == 3 else None)
        return (
            remote(a, a, or_send.at[s], ol_recv.at[s], up),
            remote(b, b, ol_send.at[s], or_recv.at[s], down),
        )

    def out_step(s):
        lo, hi = lax.rem(z + 8 - s, 8), lax.rem(z + s, 8)
        landed(out_at(lo, 0 if s == 4 else None), ol_recv.at[s - 1])
        landed(out_at(hi, 1 if s == 4 else None), or_recv.at[s - 1])
        if s < 4:
            for copy in out_sends(s):
                send(copy)

    def swap_copy(d):
        block = lax.rem(head + d, 8)
        target = wo.at[:, head, dp]
        return remote(
            ring.at[block], target, swap_send.at[d], swap_recv.at[8 - d], (dp, z, block)
        )

    swap_own = pltpu.make_async_copy(ring.at[head], wo.at[:, head, dp], swap_recv.at[0])

    def swap():
        for d in range(1, 8):
            swap_copy(d).start()
        swap_own.start()

    def share_copy(i):
        part = wo.at[:, :, mates[1][0] if i == 2 else dp]
        return remote(part, part, share_send.at[i], share_recv.at[i], mates[i % 2])

    def share():
        for d in range(8):
            landed(wo.at[:, lax.rem(head + d, 8), dp], swap_recv.at[d])
        for i in range(2):
            share_copy(i).start()

    def share_on():
        landed(wo.at[:, :, mates[1][0]], share_recv.at[1])
        share_copy(2).start()

    def share_wait():
        landed(wo.at[:, :, mates[0][0]], share_recv.at[0])
        landed(wo.at[:, :, mates[2][0]], share_recv.at[2])

    own = [
        pltpu.make_async_copy(video, tok.at[pl.ds(0, VROWS), cols_of(head)], local_sem.at[0]),
        pltpu.make_async_copy(
            text, tok.at[pl.ds(VROWS, ROWS - VROWS), cols_of(head)], local_sem.at[1]
        ),
        pltpu.make_async_copy(quarter, ring.at[z], local_sem.at[2]),
    ]
    block_rows = pl.ds(pl.multiple_of(z * WIDTH, WIDTH), WIDTH)
    own_queries, own_quarters = [], []
    for p in range(3):
        own.append(
            pltpu.make_async_copy(
                w_qkv.at[:, w_cols(p)],
                wkv.at[block_rows, pl.ds(256 * p, 256)],
                local_sem.at[3 + p],
            )
        )
        own_queries.append(
            pltpu.make_async_copy(
                w_qkv.at[:, w_cols(3 + p)],
                q_block.at[:, pl.ds(128 * p, 128)],
                local_sem.at[6 + p],
            )
        )
    for i, quarter_of in enumerate((dp, mates[0][0], mates[1][0])):
        rows = pl.ds(pl.multiple_of(quarter_of * 96, 96), 96)
        own_quarters.append(
            pltpu.make_async_copy(q_block.at[rows], wq.at[z, quarter_of], local_sem.at[15 + i])
        )
    small = [
        pltpu.make_async_copy(a, b, local_sem.at[9 + i])
        for i, (a, b) in enumerate(
            (
                (freqs_in, freqs),
                (shift_in, shift),
                (scale_in, scale),
                (q_gain_in, q_gain),
                (k_gain_in, k_gain),
                (gate_in.at[:, cols_of(head)], gate),
            )
        )
    ]
    for copy in own_queries:
        copy.start()
    for p in range(3):
        ring_first(p)
    for t in range(5):
        stage0(t)
    for copy in small + own:
        copy.start()
    for copy in small:
        copy.wait()

    def query_first():
        src = q_block.at[pl.ds(pl.multiple_of(dp * 96, 96), 96)]
        send(remote(src, wq.at[z, dp], wr_send.at[3, 0], wl_recv.at[3, 0], up))
        send(remote(src, wq.at[z, dp], wl_send.at[3, 0], wr_recv.at[3, 0], down))

    e0 = lengths[0]
    e1 = e0 + lengths[1]
    e2 = e1 + lengths[2]

    def clips(place, is_video, owner):
        ids = (
            (place >= e0).astype(jnp.int32)
            + (place >= e1).astype(jnp.int32)
            + (place >= e2).astype(jnp.int32)
        )
        return jnp.where(is_video, ids, owner)

    def tables(t):
        rows = pl.ds(t * TILE, TILE)
        row = lax.broadcasted_iota(jnp.int32, (TILE, HD), 0) + t * TILE
        place = z * VROWS + row
        q_clip[rows, :] = clips(place, row < VROWS, owners[z // 2])
        start = jnp.where(place >= e0, e0, 0)
        start = jnp.where(place >= e1, e1, start)
        start = jnp.where(place >= e2, e2, start)
        place = jnp.where(row < VROWS, place - start, 0).astype(F32)
        angle = place * freqs[...]
        lane = lax.broadcasted_iota(jnp.int32, (TILE, HD), 1)
        sine = jnp.sin(angle)
        cos_t[rows, :] = jnp.cos(angle)
        sin_t[rows, :] = jnp.where(lane < HD // 2, -sine, sine)

    def rms_rope(value, gain):
        mean = jnp.sum(value * value, axis=1, keepdims=True) * (1.0 / HD)
        value = value * lax.rsqrt(mean + 1e-06) * gain
        return value * cos_t[...] + pltpu.roll(value, HD // 2, 1) * sin_t[...]

    def ring_steps(s, *pieces):
        for p in pieces:
            if p == 4:
                out_step(s)
            elif p == 3:
                q_step(s)
            else:
                ring_step(p, s)

    for t in range(5):
        tables(t)
        stage1(t)
        if t < 3:
            ring_steps(1, t)
    for copy in own_queries:
        copy.wait()
    for copy in own_quarters:
        copy.start()
    query_first()
    out_first()
    for t in range(5):
        stage2(t)
        if t < 3:
            ring_steps(2, t)
    for copy in own + own_quarters:
        copy.wait()
    ring_steps(1, 3, 4)
    stage3(0)
    ring_steps(3, 0, 1, 2)
    stage3(1)
    ring_steps(2, 3, 4)
    stage3(2)
    ring_steps(4, 0, 1, 2)
    ring_steps(3, 3, 4)
    stage3(3)
    stage3(4)
    sib_wait(0)

    def own_sends(h):
        for i in range(2):
            a, b = kvbuf.at[h, z, i], kvbuf.at[h, z, 1 - i]
            remote(a, a, right_send.at[h, i], left_recv.at[h, i], up).start()
            remote(b, b, left_send.at[h, i], right_recv.at[h, i], down).start()

    def pass_on(h, j):
        odd = lax.rem(j, 2)
        lo, hi = lax.rem(z + 7 - j // 2, 8), lax.rem(z + 1 + j // 2, 8)
        from_left, from_right = kvbuf.at[h, lo, odd], kvbuf.at[h, hi, 1 - odd]
        landed(from_left, left_recv.at[h, j])

        @pl.when(j < 5)
        def _():
            remote(
                from_left, from_left, right_send.at[h, j + 2], left_recv.at[h, j + 2], up
            ).start()

        landed(from_right, right_recv.at[h, j])

        @pl.when(j < 5)
        def _():
            remote(
                from_right, from_right, left_send.at[h, j + 2], right_recv.at[h, j + 2], down
            ).start()

    for h in range(3):
        kv = jnp.dot(mod[...], wkv[:, 256 * h : 256 * h + 256], preferred_element_type=F32)
        keys = rms_rope(kv[:, 0:HD], k_gain[...]).astype(BF)
        values = kv[:, HD : 2 * HD].astype(BF)
        for i in range(2):
            rows = slice(i * (ROWS // 2), (i + 1) * (ROWS // 2))
            kvbuf[h, z, i, :, 0:HD] = keys[rows]
            kvbuf[h, z, i, :, HD : 2 * HD] = values[rows]
        if h == 0:
            own_sends(0)
            ring_steps(4, 3, 4)
            q_on()
            swap()
            sib_wait(1)
            sib_wait(2)
        elif h == 1:
            own_sends(1)
            pass_on(0, 0)
    q_wait()
    pass_on(0, 1)
    queries = jnp.dot(mod[...], wq[...].reshape(3072, WIDTH), preferred_element_type=F32)
    for h in range(3):
        q[h] = rms_rope(queries[:, h * HD : (h + 1) * HD], q_gain[...]).astype(BF)
    proj[...] = jnp.zeros_like(proj)

    factor = math.log2(math.e) / math.sqrt(HD)
    mine = pl.ds(pl.multiple_of(head * HD, HD), HD)

    def unit(h, b, first, each=None):
        keys = kvbuf[h, b, :, :, 0:HD].reshape(ROWS, HD)
        values = kvbuf[h, b, :, :, HD : 2 * HD].reshape(ROWS, HD)
        column = lax.broadcasted_iota(jnp.int32, (1, ROWS), 1)
        key_clip = clips(b * VROWS + column, column < VROWS, owners[b // 2])
        tiles = [pl.ds(t * TILE, TILE) for t in range(5)]

        def score(rows):
            return lax.dot_general(
                q[h, rows, :], keys, (((1,), (1,)), ((), ())), preferred_element_type=F32
            )

        def weigh(rows, scores):
            scores = jnp.where(q_clip[rows, 0:1] == key_clip, scores, -1e30)
            old = jnp.where(first, -1e30, best[rows, 0:1])
            newest = jnp.maximum(old, jnp.max(scores, axis=1, keepdims=True))
            best[rows, :] = jnp.broadcast_to(newest, (TILE, HD))
            return jnp.exp2((scores - newest) * factor), jnp.exp2((old - newest) * factor)

        def absorb(rows, weights, keep):
            count = jnp.sum(weights, axis=1, keepdims=True)
            summed = jnp.dot(weights.astype(BF), values, preferred_element_type=F32)
            prior = jnp.where(first, 0.0, total[rows, 0:1])
            before = jnp.where(first, 0.0, acc[rows, :])
            total[rows, :] = jnp.broadcast_to(prior * keep + count, (TILE, HD))
            acc[rows, :] = before * keep + summed

        scored = [score(rows) for rows in tiles]
        if each is None:
            weighed = [weigh(rows, scores) for rows, scores in zip(tiles, scored)]
            for rows, pair in zip(tiles, weighed):
                absorb(rows, *pair)
        else:
            for t, rows in enumerate(tiles):
                absorb(rows, *weigh(rows, scored[t]))
                each(t)

    def att_copy(h, d):
        part = att.at[h, :, mine]
        return remote(part, part, att_send.at[h, d], att_recv.at[h, 8 - d], peers[d - 1])

    def finish(h):
        att[h, :, mine] = (acc[...] / total[...]).astype(BF)
        for d in range(1, 8):
            att_copy(h, d).start()

    def from_peer(d):
        return pl.ds(pl.multiple_of(lax.rem(head + d, 8) * HD, HD), HD)

    def out_project(h):
        for d in range(1, 8):
            landed(att.at[h, :, from_peer(d)], att_recv.at[h, d])
        proj[...] += jnp.dot(att[h], wo[h].reshape(8 * HD, WIDTH), preferred_element_type=F32)

    def last_copy(t, d):
        part = att.at[2, pl.ds(t * TILE, TILE), mine]
        return remote(part, part, last_send.at[t, d], last_recv.at[t, 8 - d], peers[d - 1])

    def finish_tile(t):
        rows = pl.ds(t * TILE, TILE)
        att[2, rows, mine] = (acc[rows, :] / total[rows, :]).astype(BF)
        for d in range(1, 8):
            last_copy(t, d).start()

    def step(t, carry):
        h, j = t // 7, lax.rem(t, 7)
        odd = lax.rem(j, 2)

        @pl.when(t >= 2)
        def _():
            pass_on(h, j)

        @pl.when(t == 4)
        def _():
            own_sends(2)

        @pl.when(t == 1)
        def _():
            share()

        @pl.when(t == 8)
        def _():
            share_on()

        away = jnp.where(j == 6, 4, (j + 1) // 2)
        unit(h, lax.rem(jnp.where(odd == 1, z + 8 - away, z + away), 8), j == 0)

        @pl.when(j == 5)
        def _():
            unit(h, lax.rem(z + 3, 8), False)

        @pl.when(j == 6)
        def _():
            finish(h)

        @pl.when(t == 17)
        def _():
            share_wait()
            out_project(0)

        @pl.when(t == 19)
        def _():
            out_project(1)

        return carry

    lax.fori_loop(0, 20, step, 0)
    pass_on(2, 6)
    unit(2, lax.rem(z + 4, 8), False, finish_tile)
    weights_out = wo[2].reshape(8 * HD, WIDTH)
    for t in range(5):
        rows = pl.ds(t * TILE, TILE)
        for d in range(1, 8):
            landed(att.at[2, rows, from_peer(d)], last_recv.at[t, d])
        summed = proj[rows, :] + jnp.dot(att[2, rows, :], weights_out, preferred_element_type=F32)
        residual = tok[rows, cols_of(head)].astype(F32)
        result = (residual + gate[...] * summed).astype(BF)
        if t < 4:
            video_out[rows, :] = result
        else:
            text_out[...] = result

    def drain(t, carry):
        h, j = t // 7, lax.rem(t, 7)
        part = kvbuf.at[h, z, 0]
        remote(part, part, right_send.at[h, j], left_recv.at[h, j], up).wait_send()
        remote(part, part, left_send.at[h, j], right_recv.at[h, j], down).wait_send()
        return carry

    lax.fori_loop(0, 21, drain, 0)
    for d in range(1, 8):
        swap_copy(d).wait_send()
        for h in range(2):
            att_copy(h, d).wait_send()
        for t in range(5):
            last_copy(t, d).wait_send()
    for i in range(3):
        share_copy(i).wait_send()
    for copy in sends:
        copy.wait_send()


def on_device(
    video, text, shift, scale, gate, w_qkv, w_out, q_gain, k_gain, clip_lengths, text_owner
):
    anywhere = pl.BlockSpec(memory_space=pl.ANY)
    vmem = pl.BlockSpec(memory_space=pltpu.VMEM)
    smem = pl.BlockSpec(memory_space=pltpu.SMEM)
    dma = pltpu.SemaphoreType.DMA
    exponents = np.arange(HD // 2, dtype=np.float64) * (-2.0 / HD)
    freqs = np.tile((10000.0**exponents).astype(np.float32), 2).reshape(1, HD)
    return pl.pallas_call(
        sublayer_kernel,
        name="sublayer",
        out_shape=(
            jax.ShapeDtypeStruct((VROWS, WIDTH), BF),
            jax.ShapeDtypeStruct((ROWS - VROWS, WIDTH), BF),
        ),
        in_specs=[anywhere] * 10 + [smem] * 2,
        out_specs=(vmem, vmem),
        scratch_shapes=[
            pltpu.VMEM((ROWS, 3072), BF),
            pltpu.VMEM((ROWS, 3072), BF),
            pltpu.VMEM((3072, 768), BF),
            pltpu.VMEM((8, 4, 96, WIDTH), BF),
            pltpu.VMEM((8, 3, 32, WIDTH), BF),
            pltpu.VMEM((3, 8, 4, 32, WIDTH), BF),
            pltpu.VMEM((ROWS, HD), F32),
            pltpu.VMEM((ROWS, HD), F32),
            pltpu.VMEM((1, 3072), F32),
            pltpu.VMEM((1, 3072), F32),
            pltpu.VMEM((1, WIDTH), F32),
            pltpu.VMEM((1, HD), F32),
            pltpu.VMEM((1, HD), F32),
            pltpu.VMEM((1, HD), F32),
            pltpu.VMEM((WIDTH, WIDTH), BF),
            pltpu.VMEM((3, ROWS, HD), BF),
            pltpu.VMEM((3, 8, 2, ROWS // 2, 2 * HD), BF),
            pltpu.VMEM((3, ROWS, 8 * HD), BF),
            pltpu.VMEM((ROWS, WIDTH), F32),
            pltpu.VMEM((ROWS, HD), F32),
            pltpu.VMEM((ROWS, HD), F32),
            pltpu.VMEM((ROWS, HD), F32),
            pltpu.VMEM((ROWS, HD), jnp.int32),
            dma((18,)),
            dma((2, 4, 5, 3)),
            dma((64,)),
            dma((4, 4)),
            dma((4, 4)),
            dma((4, 4)),
            dma((4, 4)),
            dma((3, 8)),
            dma((3, 8)),
            dma((3, 8)),
            dma((3, 8)),
            dma((4,)),
            dma((4,)),
            dma((4,)),
            dma((4,)),
            dma((8,)),
            dma((8,)),
            dma((3,)),
            dma((3,)),
            dma((3, 7)),
            dma((3, 7)),
            dma((3, 7)),
            dma((3, 7)),
            dma((2, 8)),
            dma((2, 8)),
            dma((5, 8)),
            dma((5, 8)),
        ],
        compiler_params=pltpu.CompilerParams(
            collective_id=1, has_side_effects=True, vmem_limit_bytes=60 * 2**20
        ),
    )(
        video,
        text,
        w_qkv,
        w_out.reshape(3, 128, WIDTH),
        shift.reshape(1, -1),
        scale.reshape(1, -1),
        gate.reshape(1, -1),
        q_gain.reshape(1, HD),
        k_gain.reshape(1, HD),
        jnp.asarray(freqs),
        clip_lengths,
        text_owner,
    )


def solution(mesh):
    return jax.shard_map(
        on_device,
        mesh=mesh,
        in_specs=(
            P(("dp", "blk"), "head"),
            P(("dp", "blk"), "head"),
            P(),
            P(),
            P(),
            P("blk", "head"),
            P("head", "blk"),
            P(),
            P(),
            P("dp"),
            P("dp"),
        ),
        out_specs=(P(("dp", "blk"), "head"), P(("dp", "blk"), "head")),
        check_vma=False,
    )
```

```python
import functools
import math

import jax
import jax.numpy as jnp
import numpy as np
from jax import lax
from jax.experimental import pallas as pl
from jax.experimental.pallas import tpu as pltpu
from jax.sharding import PartitionSpec as P

MESH = pl.DeviceIdType.MESH
BF = jnp.bfloat16
F32 = jnp.float32
ROWS = 640
VROWS = 512
WIDTH = 384
HD = 128
TILE = 128


def remote(src, dst, send_sem, recv_sem, device):
    return pltpu.make_async_remote_copy(
        src_ref=src,
        dst_ref=dst,
        send_sem=send_sem,
        recv_sem=recv_sem,
        device_id=device,
        device_id_type=MESH,
    )


def greet(devices):
    barrier = pltpu.get_barrier_semaphore()
    for device in devices:
        pl.semaphore_signal(barrier, inc=1, device_id=device, device_id_type=MESH)
    pl.semaphore_wait(barrier, len(devices))


PARTS = {
    "all": (0, 128, 0),
    "f0": (0, 64, 0),
    "f1": (64, 64, 1),
    "a": (0, 80, 0),
    "b": (80, 48, 1),
    "a0": (0, 48, 0),
    "a1": (48, 32, 2),
}


def sublayer_kernel(
    video,
    text,
    w_qkv,
    w_out,
    shift_in,
    scale_in,
    gate_in,
    q_gain_in,
    k_gain_in,
    freqs_in,
    lengths,
    owners,
    video_out,
    text_out,
    tok,
    mod,
    wkv,
    wq,
    ring,
    wo,
    cos_t,
    sin_t,
    shift,
    scale,
    gate,
    q_gain,
    k_gain,
    freqs,
    q_block,
    q,
    kvbuf,
    att,
    proj,
    best,
    total,
    acc,
    q_clip,
    local_sem,
    tok_recv,
    tok_send,
    wl_recv,
    wr_recv,
    wr_send,
    wl_send,
    sib_recv,
    sib_send,
    q_recv,
    q_send,
    ol_recv,
    or_recv,
    or_send,
    ol_send,
    swap_recv,
    swap_send,
    share_recv,
    share_send,
    left_recv,
    right_recv,
    right_send,
    left_send,
    att_recv,
    att_send,
    last_recv,
    last_send,
):
    dp, z, head = lax.axis_index("dp"), lax.axis_index("blk"), lax.axis_index("head")
    core = lax.rem(dp, 2)
    yh, x = head // 4, lax.rem(head, 4)
    sibling = (dp + 1 - 2 * core, z, head)
    mates = [sibling] + [
        (d, z, head) for d in (lax.rem(dp + 2, 4), lax.rem(dp + 2, 4) + 1 - 2 * core)
    ]
    up, down = (dp, lax.rem(z + 1, 8), head), (dp, lax.rem(z + 7, 8), head)
    xs = [lax.rem(x + d, 4) for d in range(4)]
    slot = [[yh * 4 + xs[d] for d in range(4)], [(1 - yh) * 4 + xs[d] for d in range(4)]]
    right, left, over = (dp, z, slot[0][1]), (dp, z, slot[0][3]), (dp, z, slot[1][0])
    peers = [(dp, z, lax.rem(head + d, 8)) for d in range(1, 8)]
    greet(peers + [up, down] + mates)

    sends = []

    def send(copy):
        copy.start()
        sends.append(copy)

    def landed(ref, sem):
        pltpu.make_async_copy(ref, ref, sem).wait()

    def cols_of(h):
        return pl.ds(pl.multiple_of(h * WIDTH, WIDTH), WIDTH)

    def tok_at(h, t, part):
        first, count, _ = PARTS[part]
        return tok.at[pl.ds(t * TILE + first, count), cols_of(h)]

    def own_tile(t):
        return video.at[pl.ds(t * TILE, TILE)] if t < 4 else text.at[pl.ds(0, TILE)]

    send_count = [0]

    def tok_copy(src, h, t, part, flip, dx, device):
        index = send_count[0]
        send_count[0] += 1
        arrival = tok_recv.at[flip, dx, t, PARTS[part][2]]
        send(remote(src, tok_at(h, t, part), tok_send.at[index], arrival, device))

    def tok_pass(h, t, part, flip, dx, device):
        tok_copy(tok_at(h, t, part), h, t, part, flip, dx, device)

    def tok_wait(flip, dx, t, part):
        landed(tok_at(slot[flip][dx], t, part), tok_recv.at[flip, dx, t, PARTS[part][2]])

    def stage0(t):
        tok_copy(own_tile(t), head, t, "all", 0, 3, right)
        tok_copy(own_tile(t), head, t, "all", 0, 1, left)
        tok_copy(own_tile(t), head, t, "all", 1, 0, over)

    def stage1(t):
        tok_wait(1, 0, t, "all")
        tok_pass(slot[1][0], t, "a", 1, 3, right)
        tok_pass(slot[1][0], t, "a", 1, 1, left)
        for dx, part, device in ((3, "f0", right), (1, "f1", left)):
            tok_wait(0, dx, t, "all")
            tok_pass(slot[0][dx], t, part, 0, 2, device)
            tok_pass(slot[0][dx], t, "b", 1, dx, over)

    def stage2(t):
        for dx, part, device in ((3, "a0", right), (1, "a1", left)):
            tok_wait(1, dx, t, "a")
            tok_pass(slot[1][dx], t, part, 1, 2, device)
        tok_wait(0, 2, t, "f0")
        tok_wait(0, 2, t, "f1")
        tok_pass(slot[0][2], t, "b", 1, 2, over)

    def stage3(t):
        for dx, part in ((2, "a0"), (2, "a1"), (1, "b"), (3, "b"), (2, "b")):
            tok_wait(1, dx, t, part)
        normalise(t)

    def normalise(t):
        @pl.loop(0, 8, unroll=4)
        def _(i):
            rows = pl.ds(pl.multiple_of(t * TILE + i * 16, 16), 16)
            value = tok[rows, :].astype(F32)
            mean = jnp.sum(value, axis=1, keepdims=True) * (1.0 / 3072.0)
            value = value - mean
            var = jnp.sum(value * value, axis=1, keepdims=True) * (1.0 / 3072.0)
            value = value * lax.rsqrt(var + 1e-06) * (1.0 + scale[...]) + shift[...]
            mod[rows, :] = value.astype(BF)

    def w_at(block, p, half=None, side=None):
        first, count = (0, 192) if half is None else (half * 96, 96)
        side = core if side is None else side
        rows = pl.ds(pl.multiple_of(block * WIDTH + side * 192 + first, 32), count)
        return wkv.at[rows, pl.ds(256 * p, 256)]

    def w_cols(p):
        return pl.ds(384 * p + 128, 256) if p < 3 else pl.ds(384 * (p - 3), 128)

    def ring_first(p):
        src = w_qkv.at[pl.ds(pl.multiple_of(core * 192, 192), 192), w_cols(p)]
        send(remote(src, w_at(z, p), wr_send.at[p, 0], wl_recv.at[p, 0], up))
        send(remote(src, w_at(z, p), wl_send.at[p, 0], wr_recv.at[p, 0], down))

    def ring_step(p, s):
        lo, hi = lax.rem(z + 8 - s, 8), lax.rem(z + s, 8)
        half_a, half_b = (0, 1) if s == 4 else (None, None)
        landed(w_at(lo, p, half_a), wl_recv.at[p, s - 1])
        if s < 4:
            src = w_at(lo, p, 0 if s == 3 else None)
            send(remote(src, src, wr_send.at[p, s], wl_recv.at[p, s], up))
        landed(w_at(hi, p, half_b), wr_recv.at[p, s - 1])
        if s < 4:
            src = w_at(hi, p, 1 if s == 3 else None)
            send(remote(src, src, wl_send.at[p, s], wr_recv.at[p, s], down))
        for i, (block, half) in enumerate(((lo, half_a), (hi, half_b))):
            ref = w_at(block, p, half)
            k = 2 * (s - 1) + i
            send(remote(ref, ref, sib_send.at[p, k], sib_recv.at[p, k], sibling))

    def sib_wait(p):
        for s in range(1, 5):
            for i in range(2):
                block = lax.rem(z + 8 - s, 8) if i == 0 else lax.rem(z + s, 8)
                ref = w_at(block, p, i if s == 4 else None, 1 - core)
                landed(ref, sib_recv.at[p, 2 * (s - 1) + i])

    def q_at(block, half, quarter):
        part = wq.at[block, quarter]
        return part if half is None else part.at[pl.ds(half * 48, 48)]

    def q_pair(s, quarter, split):
        lo, hi = lax.rem(z + 8 - s, 8), lax.rem(z + s, 8)
        return q_at(lo, 0 if split else None, quarter), q_at(hi, 1 if split else None, quarter)

    def q_sends(s):
        a, b = q_pair(s, dp, s == 3)
        send(remote(a, a, wr_send.at[3, s], wl_recv.at[3, s], up))
        send(remote(b, b, wl_send.at[3, s], wr_recv.at[3, s], down))

    def q_step(s):
        a, b = q_pair(s, dp, s == 4)
        landed(a, wl_recv.at[3, s - 1])
        landed(b, wr_recv.at[3, s - 1])
        if s < 4:
            q_sends(s)
        for i in range(2):
            for k, ref in enumerate((a, b)):
                n = 2 * (s - 1) + k
                send(remote(ref, ref, q_send.at[i, n], q_recv.at[i, n], mates[i]))

    def q_on():
        for s in range(1, 5):
            for k, ref in enumerate(q_pair(s, mates[1][0], s == 4)):
                landed(ref, q_recv.at[1, 2 * (s - 1) + k])
        part = wq.at[:, mates[1][0]]
        send(remote(part, part, q_send.at[2, 0], q_recv.at[2, 0], sibling))

    def q_wait():
        for s in range(1, 5):
            for k, ref in enumerate(q_pair(s, sibling[0], s == 4)):
                landed(ref, q_recv.at[0, 2 * (s - 1) + k])
        landed(wq.at[:, mates[2][0]], q_recv.at[2, 0])

    quarter = w_out.at[:, pl.ds(pl.multiple_of(dp * 32, 32), 32)]

    def out_first():
        send(remote(quarter, ring.at[z], or_send.at[0], ol_recv.at[0], up))
        send(remote(quarter, ring.at[z], ol_send.at[0], or_recv.at[0], down))

    def out_at(block, half):
        return ring.at[block] if half is None else ring.at[block, :, pl.ds(half * 16, 16)]

    def out_sends(s):
        lo, hi = lax.rem(z + 8 - s, 8), lax.rem(z + s, 8)
        a, b = out_at(lo, 0 if s == 3 else None), out_at(hi, 1 if s == 3 else None)
        return (
            remote(a, a, or_send.at[s], ol_recv.at[s], up),
            remote(b, b, ol_send.at[s], or_recv.at[s], down),
        )

    def out_step(s):
        lo, hi = lax.rem(z + 8 - s, 8), lax.rem(z + s, 8)
        landed(out_at(lo, 0 if s == 4 else None), ol_recv.at[s - 1])
        landed(out_at(hi, 1 if s == 4 else None), or_recv.at[s - 1])
        if s < 4:
            for copy in out_sends(s):
                send(copy)

    def swap_copy(d):
        block = lax.rem(head + d, 8)
        target = wo.at[:, head, dp]
        return remote(
            ring.at[block], target, swap_send.at[d], swap_recv.at[8 - d], (dp, z, block)
        )

    swap_own = pltpu.make_async_copy(ring.at[head], wo.at[:, head, dp], swap_recv.at[0])

    def swap():
        for d in range(1, 8):
            swap_copy(d).start()
        swap_own.start()

    def share_copy(i):
        part = wo.at[:, :, mates[1][0] if i == 2 else dp]
        return remote(part, part, share_send.at[i], share_recv.at[i], mates[i % 2])

    def share():
        for d in range(8):
            landed(wo.at[:, lax.rem(head + d, 8), dp], swap_recv.at[d])
        for i in range(2):
            share_copy(i).start()

    def share_on():
        landed(wo.at[:, :, mates[1][0]], share_recv.at[1])
        share_copy(2).start()

    def share_wait():
        landed(wo.at[:, :, mates[0][0]], share_recv.at[0])
        landed(wo.at[:, :, mates[2][0]], share_recv.at[2])

    own = [
        pltpu.make_async_copy(video, tok.at[pl.ds(0, VROWS), cols_of(head)], local_sem.at[0]),
        pltpu.make_async_copy(
            text, tok.at[pl.ds(VROWS, ROWS - VROWS), cols_of(head)], local_sem.at[1]
        ),
        pltpu.make_async_copy(quarter, ring.at[z], local_sem.at[2]),
    ]
    block_rows = pl.ds(pl.multiple_of(z * WIDTH, WIDTH), WIDTH)
    own_queries, own_quarters = [], []
    for p in range(3):
        own.append(
            pltpu.make_async_copy(
                w_qkv.at[:, w_cols(p)],
                wkv.at[block_rows, pl.ds(256 * p, 256)],
                local_sem.at[3 + p],
            )
        )
        own_queries.append(
            pltpu.make_async_copy(
                w_qkv.at[:, w_cols(3 + p)],
                q_block.at[:, pl.ds(128 * p, 128)],
                local_sem.at[6 + p],
            )
        )
    for i, quarter_of in enumerate((dp, mates[0][0], mates[1][0])):
        rows = pl.ds(pl.multiple_of(quarter_of * 96, 96), 96)
        own_quarters.append(
            pltpu.make_async_copy(q_block.at[rows], wq.at[z, quarter_of], local_sem.at[15 + i])
        )
    small = [
        pltpu.make_async_copy(a, b, local_sem.at[9 + i])
        for i, (a, b) in enumerate(
            (
                (freqs_in, freqs),
                (shift_in, shift),
                (scale_in, scale),
                (q_gain_in, q_gain),
                (k_gain_in, k_gain),
                (gate_in.at[:, cols_of(head)], gate),
            )
        )
    ]
    for copy in own_queries:
        copy.start()
    for p in range(3):
        ring_first(p)
    for t in range(5):
        stage0(t)
    for copy in small + own:
        copy.start()
    for copy in small:
        copy.wait()

    def query_first():
        src = q_block.at[pl.ds(pl.multiple_of(dp * 96, 96), 96)]
        send(remote(src, wq.at[z, dp], wr_send.at[3, 0], wl_recv.at[3, 0], up))
        send(remote(src, wq.at[z, dp], wl_send.at[3, 0], wr_recv.at[3, 0], down))

    e0 = lengths[0]
    e1 = e0 + lengths[1]
    e2 = e1 + lengths[2]

    def clips(place, is_video, owner):
        ids = (
            (place >= e0).astype(jnp.int32)
            + (place >= e1).astype(jnp.int32)
            + (place >= e2).astype(jnp.int32)
        )
        return jnp.where(is_video, ids, owner)

    def tables(t):
        rows = pl.ds(t * TILE, TILE)
        row = lax.broadcasted_iota(jnp.int32, (TILE, HD), 0) + t * TILE
        place = z * VROWS + row
        q_clip[rows, :] = clips(place, row < VROWS, owners[z // 2])
        start = jnp.where(place >= e0, e0, 0)
        start = jnp.where(place >= e1, e1, start)
        start = jnp.where(place >= e2, e2, start)
        place = jnp.where(row < VROWS, place - start, 0).astype(F32)
        angle = place * freqs[...]
        lane = lax.broadcasted_iota(jnp.int32, (TILE, HD), 1)
        sine = jnp.sin(angle)
        cos_t[rows, :] = jnp.cos(angle)
        sin_t[rows, :] = jnp.where(lane < HD // 2, -sine, sine)

    def rms_rope(value, gain):
        mean = jnp.sum(value * value, axis=1, keepdims=True) * (1.0 / HD)
        value = value * lax.rsqrt(mean + 1e-06) * gain
        return value * cos_t[...] + pltpu.roll(value, HD // 2, 1) * sin_t[...]

    def ring_steps(s, *pieces):
        for p in pieces:
            if p == 4:
                out_step(s)
            elif p == 3:
                q_step(s)
            else:
                ring_step(p, s)

    for t in range(5):
        tables(t)
        stage1(t)
        if t < 3:
            ring_steps(1, t)
    for copy in own_queries:
        copy.wait()
    for copy in own_quarters:
        copy.start()
    query_first()
    out_first()
    for t in range(5):
        stage2(t)
        if t < 3:
            ring_steps(2, t)
    for copy in own + own_quarters:
        copy.wait()
    ring_steps(1, 3, 4)
    stage3(0)
    ring_steps(3, 0, 1, 2)
    stage3(1)
    ring_steps(2, 3, 4)
    stage3(2)
    ring_steps(4, 0, 1, 2)
    ring_steps(3, 3, 4)
    stage3(3)
    stage3(4)
    sib_wait(0)

    def own_sends(h):
        for i in range(2):
            a, b = kvbuf.at[h, z, i], kvbuf.at[h, z, 1 - i]
            remote(a, a, right_send.at[h, i], left_recv.at[h, i], up).start()
            remote(b, b, left_send.at[h, i], right_recv.at[h, i], down).start()

    def pass_on(h, j):
        odd = lax.rem(j, 2)
        lo, hi = lax.rem(z + 7 - j // 2, 8), lax.rem(z + 1 + j // 2, 8)
        from_left, from_right = kvbuf.at[h, lo, odd], kvbuf.at[h, hi, 1 - odd]
        landed(from_left, left_recv.at[h, j])

        @pl.when(j < 5)
        def _():
            remote(
                from_left, from_left, right_send.at[h, j + 2], left_recv.at[h, j + 2], up
            ).start()

        landed(from_right, right_recv.at[h, j])

        @pl.when(j < 5)
        def _():
            remote(
                from_right, from_right, left_send.at[h, j + 2], right_recv.at[h, j + 2], down
            ).start()

    for h in range(3):
        kv = jnp.dot(mod[...], wkv[:, 256 * h : 256 * h + 256], preferred_element_type=F32)
        keys = rms_rope(kv[:, 0:HD], k_gain[...]).astype(BF)
        values = kv[:, HD : 2 * HD].astype(BF)
        for i in range(2):
            rows = slice(i * (ROWS // 2), (i + 1) * (ROWS // 2))
            kvbuf[h, z, i, :, 0:HD] = keys[rows]
            kvbuf[h, z, i, :, HD : 2 * HD] = values[rows]
        if h == 0:
            own_sends(0)
            ring_steps(4, 3, 4)
            q_on()
            swap()
            sib_wait(1)
            sib_wait(2)
        elif h == 1:
            own_sends(1)
            pass_on(0, 0)
    q_wait()
    pass_on(0, 1)
    queries = jnp.dot(mod[...], wq[...].reshape(3072, WIDTH), preferred_element_type=F32)
    for h in range(3):
        q[h] = rms_rope(queries[:, h * HD : (h + 1) * HD], q_gain[...]).astype(BF)
    proj[...] = jnp.zeros_like(proj)

    factor = math.log2(math.e) / math.sqrt(HD)
    mine = pl.ds(pl.multiple_of(head * HD, HD), HD)

    def unit(h, b, first, each=None):
        keys = kvbuf[h, b, :, :, 0:HD].reshape(ROWS, HD)
        values = kvbuf[h, b, :, :, HD : 2 * HD].reshape(ROWS, HD)
        column = lax.broadcasted_iota(jnp.int32, (1, ROWS), 1)
        key_clip = clips(b * VROWS + column, column < VROWS, owners[b // 2])
        tiles = [pl.ds(t * TILE, TILE) for t in range(5)]

        def score(rows):
            return lax.dot_general(
                q[h, rows, :], keys, (((1,), (1,)), ((), ())), preferred_element_type=F32
            )

        def weigh(rows, scores):
            scores = jnp.where(q_clip[rows, 0:1] == key_clip, scores, -1e30)
            old = jnp.where(first, -1e30, best[rows, 0:1])
            newest = jnp.maximum(old, jnp.max(scores, axis=1, keepdims=True))
            best[rows, :] = jnp.broadcast_to(newest, (TILE, HD))
            return jnp.exp2((scores - newest) * factor), jnp.exp2((old - newest) * factor)

        def absorb(rows, weights, keep):
            count = jnp.sum(weights, axis=1, keepdims=True)
            summed = jnp.dot(weights.astype(BF), values, preferred_element_type=F32)
            prior = jnp.where(first, 0.0, total[rows, 0:1])
            before = jnp.where(first, 0.0, acc[rows, :])
            total[rows, :] = jnp.broadcast_to(prior * keep + count, (TILE, HD))
            acc[rows, :] = before * keep + summed

        scored = [score(rows) for rows in tiles]
        if each is None:
            weighed = [weigh(rows, scores) for rows, scores in zip(tiles, scored)]
            for rows, pair in zip(tiles, weighed):
                absorb(rows, *pair)
        else:
            for t, rows in enumerate(tiles):
                absorb(rows, *weigh(rows, scored[t]))
                each(t)

    def att_copy(h, d):
        part = att.at[h, :, mine]
        return remote(part, part, att_send.at[h, d], att_recv.at[h, 8 - d], peers[d - 1])

    def finish(h):
        att[h, :, mine] = (acc[...] / total[...]).astype(BF)
        for d in range(1, 8):
            att_copy(h, d).start()

    def from_peer(d):
        return pl.ds(pl.multiple_of(lax.rem(head + d, 8) * HD, HD), HD)

    def out_project(h):
        for d in range(1, 8):
            landed(att.at[h, :, from_peer(d)], att_recv.at[h, d])
        proj[...] += jnp.dot(att[h], wo[h].reshape(8 * HD, WIDTH), preferred_element_type=F32)

    def last_copy(t, d):
        part = att.at[2, pl.ds(t * TILE, TILE), mine]
        return remote(part, part, last_send.at[t, d], last_recv.at[t, 8 - d], peers[d - 1])

    def finish_tile(t):
        rows = pl.ds(t * TILE, TILE)
        att[2, rows, mine] = (acc[rows, :] / total[rows, :]).astype(BF)
        for flip, dx in ((1, 2), (1, 1), (1, 3), (0, 2), (1, 0), (0, 1), (0, 3)):
            target = slot[flip][dx]
            d = lax.rem(target - head + 8, 8)
            remote(
                att.at[2, rows, mine],
                att.at[2, rows, mine],
                last_send.at[t, d],
                last_recv.at[t, 8 - d],
                (dp, z, target),
            ).start()

    def step(t, carry):
        h, j = t // 7, lax.rem(t, 7)
        odd = lax.rem(j, 2)

        @pl.when(t >= 2)
        def _():
            pass_on(h, j)

        @pl.when(t == 4)
        def _():
            own_sends(2)

        @pl.when(t == 1)
        def _():
            share()

        @pl.when(t == 8)
        def _():
            share_on()

        away = jnp.where(j == 6, 4, (j + 1) // 2)
        unit(h, lax.rem(jnp.where(odd == 1, z + 8 - away, z + away), 8), j == 0)

        @pl.when(j == 5)
        def _():
            unit(h, lax.rem(z + 3, 8), False)

        @pl.when(j == 6)
        def _():
            finish(h)

        @pl.when(t == 17)
        def _():
            share_wait()
            out_project(0)

        @pl.when(t == 19)
        def _():
            out_project(1)

        return carry

    lax.fori_loop(0, 20, step, 0)
    pass_on(2, 6)
    unit(2, lax.rem(z + 4, 8), False, finish_tile)
    weights_out = wo[2].reshape(8 * HD, WIDTH)
    for t in range(5):
        rows = pl.ds(t * TILE, TILE)
        for d in range(1, 8):
            landed(att.at[2, rows, from_peer(d)], last_recv.at[t, d])
        summed = proj[rows, :] + jnp.dot(att[2, rows, :], weights_out, preferred_element_type=F32)
        residual = tok[rows, cols_of(head)].astype(F32)
        result = (residual + gate[...] * summed).astype(BF)
        if t < 4:
            video_out[rows, :] = result
        else:
            text_out[...] = result

    def drain(t, carry):
        h, j = t // 7, lax.rem(t, 7)
        part = kvbuf.at[h, z, 0]
        remote(part, part, right_send.at[h, j], left_recv.at[h, j], up).wait_send()
        remote(part, part, left_send.at[h, j], right_recv.at[h, j], down).wait_send()
        return carry

    lax.fori_loop(0, 21, drain, 0)
    for d in range(1, 8):
        swap_copy(d).wait_send()
        for h in range(2):
            att_copy(h, d).wait_send()
        for t in range(5):
            last_copy(t, d).wait_send()
    for i in range(3):
        share_copy(i).wait_send()
    for copy in sends:
        copy.wait_send()


def on_device(
    video, text, shift, scale, gate, w_qkv, w_out, q_gain, k_gain, clip_lengths, text_owner
):
    anywhere = pl.BlockSpec(memory_space=pl.ANY)
    vmem = pl.BlockSpec(memory_space=pltpu.VMEM)
    smem = pl.BlockSpec(memory_space=pltpu.SMEM)
    dma = pltpu.SemaphoreType.DMA
    exponents = np.arange(HD // 2, dtype=np.float64) * (-2.0 / HD)
    freqs = np.tile((10000.0**exponents).astype(np.float32), 2).reshape(1, HD)
    return pl.pallas_call(
        sublayer_kernel,
        name="sublayer",
        out_shape=(
            jax.ShapeDtypeStruct((VROWS, WIDTH), BF),
            jax.ShapeDtypeStruct((ROWS - VROWS, WIDTH), BF),
        ),
        in_specs=[anywhere] * 10 + [smem] * 2,
        out_specs=(vmem, vmem),
        scratch_shapes=[
            pltpu.VMEM((ROWS, 3072), BF),
            pltpu.VMEM((ROWS, 3072), BF),
            pltpu.VMEM((3072, 768), BF),
            pltpu.VMEM((8, 4, 96, WIDTH), BF),
            pltpu.VMEM((8, 3, 32, WIDTH), BF),
            pltpu.VMEM((3, 8, 4, 32, WIDTH), BF),
            pltpu.VMEM((ROWS, HD), F32),
            pltpu.VMEM((ROWS, HD), F32),
            pltpu.VMEM((1, 3072), F32),
            pltpu.VMEM((1, 3072), F32),
            pltpu.VMEM((1, WIDTH), F32),
            pltpu.VMEM((1, HD), F32),
            pltpu.VMEM((1, HD), F32),
            pltpu.VMEM((1, HD), F32),
            pltpu.VMEM((WIDTH, WIDTH), BF),
            pltpu.VMEM((3, ROWS, HD), BF),
            pltpu.VMEM((3, 8, 2, ROWS // 2, 2 * HD), BF),
            pltpu.VMEM((3, ROWS, 8 * HD), BF),
            pltpu.VMEM((ROWS, WIDTH), F32),
            pltpu.VMEM((ROWS, HD), F32),
            pltpu.VMEM((ROWS, HD), F32),
            pltpu.VMEM((ROWS, HD), F32),
            pltpu.VMEM((ROWS, HD), jnp.int32),
            dma((18,)),
            dma((2, 4, 5, 3)),
            dma((64,)),
            dma((4, 4)),
            dma((4, 4)),
            dma((4, 4)),
            dma((4, 4)),
            dma((3, 8)),
            dma((3, 8)),
            dma((3, 8)),
            dma((3, 8)),
            dma((4,)),
            dma((4,)),
            dma((4,)),
            dma((4,)),
            dma((8,)),
            dma((8,)),
            dma((3,)),
            dma((3,)),
            dma((3, 7)),
            dma((3, 7)),
            dma((3, 7)),
            dma((3, 7)),
            dma((2, 8)),
            dma((2, 8)),
            dma((5, 8)),
            dma((5, 8)),
        ],
        compiler_params=pltpu.CompilerParams(
            collective_id=1, has_side_effects=True, vmem_limit_bytes=60 * 2**20
        ),
    )(
        video,
        text,
        w_qkv,
        w_out.reshape(3, 128, WIDTH),
        shift.reshape(1, -1),
        scale.reshape(1, -1),
        gate.reshape(1, -1),
        q_gain.reshape(1, HD),
        k_gain.reshape(1, HD),
        jnp.asarray(freqs),
        clip_lengths,
        text_owner,
    )


def solution(mesh):
    return jax.shard_map(
        on_device,
        mesh=mesh,
        in_specs=(
            P(("dp", "blk"), "head"),
            P(("dp", "blk"), "head"),
            P(),
            P(),
            P(),
            P("blk", "head"),
            P("head", "blk"),
            P(),
            P(),
            P("dp"),
            P("dp"),
        ),
        out_specs=(P(("dp", "blk"), "head"), P(("dp", "blk"), "head")),
        check_vma=False,
    )
```
